128 devices in a mesh: dp: 32 (over z, x, core), tensor: 4 (over y).
Axes of the slice: x: 4, y: 4, z: 4, core: 2. Of those that a mesh axis runs over, the one named last changes fastest.
Arguments:
- acts: bfloat16 [8192, 8192], P('dp', 'tensor'), may hold values from -6 to 6
- out_grad: bfloat16 [8192, 8192], P('dp'), may hold values from -0.19921875 to 0.19921875
- basis: float32 [8192, 256], replicated, may hold values from -0.0625 to 0.0625
- moment1: float32 [4, 2048, 256], P('tensor', 'dp'), may hold values from -2 to 2
- moment2: float32 [4, 2048, 256], P('tensor', 'dp'), may hold values from 0.002 to 0.05
- weight: bfloat16 [4, 2048, 8192], P('tensor', 'dp'), may hold values from -0.0625 to 0.0625
- next_acts: bfloat16 [8192, 8192], P('dp', 'tensor'), may hold values from -6 to 6
Outputs:
- output: bfloat16 [8192, 8192], P('dp', 'tensor')
- new_weight: bfloat16 [4, 2048, 8192], P('tensor', 'dp')
- first: float32 [4, 2048, 256], P('tensor', 'dp')
- second: float32 [4, 2048, 256], P('tensor', 'dp')
The draws below stay inside these ranges and needn't reach their ends.
All inputs are finite; a program needn't handle non-finite values.
Results may differ from the reference program's by a relative error of at most 0.018.
Values may be sent and summed in bfloat16 or wider, within the bound.
No kernel may reach another device: no remote copies, remote signals or barrier semaphores. Data moves between devices by JAX's collectives and lax.ppermute only.
A program may use at most 192 MiB of HBM per device.

```python
import math
import jax
import jax.numpy as jnp
from jax import lax

D = 8192
ATTN = 8192
RANK = 256
TOKENS = 8192
N_TENSOR = 4


def level_of(own_key, shape, pieces, low, top_value):
    def one(dim, parts):
        steps = jax.random.uniform(jax.random.fold_in(jax.random.fold_in(own_key, 6), dim), (parts,), jnp.float32, low / len(pieces), top_value / len(pieces))
        return jnp.repeat(jnp.exp(steps), shape[dim] // parts).reshape((-1,) + (1,) * (len(shape) - dim - 1))

    level = one(*pieces[0])
    for cut in pieces[1:]:
        level = level * one(*cut)
    return level


def noise(own_key, extent, scale, most, split=(), held_as=jnp.bfloat16):
    gain = level_of(own_key, extent, split, -0.22, 0.18) if split else 1.0
    drawn = jax.random.normal(own_key, extent, jnp.float32) * scale * gain
    return jnp.minimum(jnp.maximum(drawn, -most), most).astype(held_as)


def setup_inputs(seed: int = 0) -> dict:
    key_of = jax.random.split(jax.random.key(seed), 8)
    acts = noise(key_of[0], (TOKENS, ATTN), 1.0, 6.0, ((0, 32), (1, 4)))
    out_grad = noise(key_of[1], (TOKENS, D), 0.03, 0.19921875, ((0, 32),))
    basis = noise(key_of[2], (D, RANK), D ** -0.5, 0.0625, (), jnp.float32)
    moment1 = noise(key_of[3], (N_TENSOR, ATTN // N_TENSOR, RANK), 0.3, 2.0, ((0, 4), (1, 32)), jnp.float32)
    moment2 = jnp.clip(jnp.exp(math.log(0.05) - 3.218876 * jax.random.uniform(key_of[4], (N_TENSOR, ATTN // N_TENSOR, RANK), jnp.float32) ** level_of(key_of[4], (N_TENSOR, ATTN // N_TENSOR, RANK), ((0, 4), (1, 32)), -0.2, 0.2)), 0.002, 0.05)
    weight = noise(key_of[5], (N_TENSOR, ATTN // N_TENSOR, D), ATTN ** -0.5, 0.0625, ((0, 4), (1, 32)))
    next_acts = noise(key_of[6], (TOKENS, ATTN), 1.0, 6.0, ((0, 32), (1, 4)))
    return {"acts": acts, "out_grad": out_grad, "basis": basis, "moment1": moment1, "moment2": moment2, "weight": weight, "next_acts": next_acts}


beta_one = 0.9
beta_two = 0.999
adam_step = 10.0
learning_rate = 0.02
epsilon = 1e-08

def reference(acts, out_grad, basis, moment1, moment2, weight, next_acts):
    rows_group = ATTN // N_TENSOR
    grad = jnp.dot(acts.T, out_grad, preferred_element_type=jnp.float32)
    projected = jnp.dot(grad, basis, precision=lax.Precision.HIGHEST, preferred_element_type=jnp.float32)
    first = beta_one * moment1.reshape(ATTN, RANK) + (1.0 - beta_one) * projected
    second = beta_two * moment2.reshape(ATTN, RANK) + (1.0 - beta_two) * projected * projected
    direction = first / (1.0 - beta_one ** adam_step) / (jnp.sqrt(second / (1.0 - beta_two ** adam_step)) + epsilon)
    change = jnp.dot(direction, basis.T, precision=lax.Precision.HIGHEST, preferred_element_type=jnp.float32)
    new_weight = (weight.reshape(ATTN, D).astype(jnp.float32) - learning_rate * change).astype(jnp.bfloat16)
    total = jnp.zeros((TOKENS, D), jnp.float32)
    for group in range(N_TENSOR):
        cols = next_acts[:, group * rows_group:(group + 1) * rows_group]
        rows = new_weight[group * rows_group:(group + 1) * rows_group]
        part = jnp.dot(cols, rows, preferred_element_type=jnp.float32).astype(jnp.bfloat16)
        total = total + part.astype(jnp.float32)
    output = total.astype(jnp.bfloat16)
    return (output, new_weight.reshape(N_TENSOR, rows_group, D), first.reshape(N_TENSOR, rows_group, RANK), second.reshape(N_TENSOR, rows_group, RANK))
```

```python
import functools

import jax
import jax.numpy as jnp
from jax import lax
from jax.experimental import pallas as pl
from jax.experimental.pallas import tpu as pltpu
from jax.sharding import Mesh
from jax.sharding import PartitionSpec as P

beta_one = 0.9
beta_two = 0.999
adam_step = 10.0
learning_rate = 0.02
epsilon = 1e-08

F32 = jnp.float32
BF16 = jnp.bfloat16
DP = ("z", "x", "c")
MIB = 1 << 20


def two_terms(value):
    high = value.astype(BF16)
    low = (value - high.astype(F32)).astype(BF16)
    return high, low


def dot(a, b):
    return jnp.dot(a, b, preferred_element_type=F32)


def dot_t(a, b, dims):
    return lax.dot_general(a, b, (dims, ((), ())), preferred_element_type=F32)


def project_kernel(grad_ref, basis_ref, acts_ref, out_ref, total):
    step = pl.program_id(0)
    high, low = two_terms(basis_ref[...])
    grad = grad_ref[...]
    term = dot(grad, high) + dot(grad, low)

    @pl.when(step == 0)
    def _():
        total[...] = term

    @pl.when(step > 0)
    def _():
        total[...] += term

    @pl.when(step == pl.num_programs(0) - 1)
    def _():
        high, low = two_terms(total[...])
        acts = acts_ref[...]
        out_ref[...] = (
            dot_t(acts, high, ((0,), (0,))) + dot_t(acts, low, ((0,), (0,)))
        ).astype(BF16)


def project(acts, out_grad, basis):
    steps = 8
    tokens, width = out_grad.shape
    rank = basis.shape[1]
    depth = width // steps
    return pl.pallas_call(
        project_kernel,
        grid=(steps,),
        in_specs=[
            pl.BlockSpec((tokens, depth), lambda i: (0, i)),
            pl.BlockSpec((depth, rank), lambda i: (i, 0)),
            pl.BlockSpec(acts.shape, lambda i: (0, 0)),
        ],
        out_specs=pl.BlockSpec((acts.shape[1], rank), lambda i: (0, 0)),
        out_shape=jax.ShapeDtypeStruct((acts.shape[1], rank), BF16),
        scratch_shapes=[pltpu.VMEM((tokens, rank), F32)],
        compiler_params=pltpu.CompilerParams(vmem_limit_bytes=48 * MIB),
        name="project",
    )(out_grad, basis, acts)


def fresh_kernel(direction_ref, basis_ref, weight_ref, out_ref):
    dh, dl = two_terms(direction_ref[...])
    bh, bl = two_terms(basis_ref[...])
    last = ((1,), (1,))
    change = dot_t(dh, bh, last) + dot_t(dh, bl, last) + dot_t(dl, bh, last)
    out_ref[...] = (weight_ref[...].astype(F32) - learning_rate * change).astype(BF16)


def fresh_rows(direction, basis, weight):
    rows, width = weight.shape
    block = 1024
    return pl.pallas_call(
        fresh_kernel,
        grid=(width // block,),
        in_specs=[
            pl.BlockSpec(direction.shape, lambda i: (0, 0)),
            pl.BlockSpec((block, basis.shape[1]), lambda i: (i, 0)),
            pl.BlockSpec((rows, block), lambda i: (0, i)),
        ],
        out_specs=pl.BlockSpec((rows, block), lambda i: (0, i)),
        out_shape=jax.ShapeDtypeStruct((rows, width), BF16),
        compiler_params=pltpu.CompilerParams(vmem_limit_bytes=48 * MIB),
        name="fresh_rows",
    )(direction, basis, weight)


def parts_kernel(place_ref, acts_ref, own, right, left, far_a, far_b, dir_ref, basis_ref, out_ref, rows):
    step = pl.program_id(0)
    depth = own.shape[0]
    half = depth // 2

    @pl.when(step == 0)
    def _():
        basis = basis_ref[...].astype(BF16)
        for piece, index, shift, size in (
            (own, 0, 0, depth),
            (right, 1, 0, depth),
            (left, 2, 0, depth),
            (far_a, 3, 0, half),
            (far_b, 3, half, half),
        ):
            at = pl.ds(pl.multiple_of(place_ref[index] * depth + shift, half), size)
            change = dot_t(dir_ref[at, :], basis, ((1,), (1,)))
            rows[at, :] = (piece[...].astype(F32) - learning_rate * change).astype(BF16)

    part = dot(acts_ref[...], rows[...]).astype(BF16)
    count, _, width = out_ref.shape
    for j in range(count):
        out_ref[j] = part[:, j * width : (j + 1) * width]


def parts(place, acts, pieces, direction, basis):
    blocks, tokens, depth = acts.shape
    columns = pieces[0].shape[1]
    whole = lambda a: pl.BlockSpec(a.shape, lambda i, place: (0,) * len(a.shape))
    return pl.pallas_call(
        parts_kernel,
        grid_spec=pltpu.PrefetchScalarGridSpec(
            num_scalar_prefetch=1,
            grid=(blocks,),
            in_specs=[
                pl.BlockSpec((None, tokens, depth), lambda i, place: (i, 0, 0)),
                *[whole(p) for p in pieces],
                whole(direction),
                whole(basis),
            ],
            out_specs=pl.BlockSpec((None, 4, tokens, columns // 4), lambda i, place: (i, 0, 0, 0)),
            scratch_shapes=[pltpu.VMEM((depth, columns), BF16)],
        ),
        out_shape=jax.ShapeDtypeStruct((blocks, 4, tokens, columns // 4), BF16),
        compiler_params=pltpu.CompilerParams(vmem_limit_bytes=56 * MIB),
        name="parts",
    )(place, acts, *pieces, direction, basis)


def shift(value, axis, by):
    return lax.ppermute(value, axis, [(i, (i + by) % 4) for i in range(4)])


def on_device(acts, out_grad, basis, moment1, moment2, weight, next_acts):
    z, x, c = lax.axis_index("z"), lax.axis_index("x"), lax.axis_index("c")
    old = weight[0]
    own = old.reshape(64, 4, 8, 256).transpose(2, 0, 1, 3).reshape(8, 64, 1024)
    own = lax.all_to_all(own, ("x", "c"), 0, 0).reshape(512, 1024)
    right = shift(own, "z", 1)
    left = shift(own, "z", -1)
    far_a = shift(right[:256], "z", 1)
    far_b = shift(left[256:], "z", -1)
    place = jnp.stack([z, (z + 3) % 4, (z + 1) % 4, (z + 2) % 4]).astype(jnp.int32)

    columns = lax.all_gather(next_acts, ("x", "c"), axis=0, tiled=False)

    projected = project(acts, out_grad, basis)
    projected = lax.all_to_all(projected.reshape(32, 64, 256), DP, 0, 0)
    projected = jnp.sum(projected.astype(F32), axis=0)
    first = beta_one * moment1[0] + (1.0 - beta_one) * projected
    second = beta_two * moment2[0] + (1.0 - beta_two) * projected * projected
    direction = (
        first
        / (1.0 - beta_one**adam_step)
        / (jnp.sqrt(second / (1.0 - beta_two**adam_step)) + epsilon)
    )
    sent = jnp.broadcast_to(direction.astype(BF16)[None], (32, 64, 256))
    directions = lax.all_to_all(sent, DP, 0, 0).reshape(2048, 256)
    fresh = fresh_rows(direction, basis, old)

    basis_rows = lax.dynamic_index_in_dim(
        basis.reshape(4, 8, 256, 256), 2 * x + c, axis=1, keepdims=False
    ).reshape(1024, 256)
    part = parts(place, columns, (own, right, left, far_a, far_b), directions, basis_rows)
    part = lax.all_to_all(part.reshape(32, 256, 256), ("x", "c", "y"), 0, 0)
    total = jnp.sum(part.reshape(8, 4, 256, 256).astype(F32), axis=1).astype(BF16)
    output = total.transpose(1, 0, 2).reshape(256, 2048)
    return (output, fresh[None], first[None], second[None])


def solution(mesh):
    cube = Mesh(mesh.devices.reshape(4, 4, 2, 4), ("z", "x", "c", "y"))
    placed = (
        P(DP, "y"),
        P(DP, None),
        P(),
        P("y", DP, None),
        P("y", DP, None),
        P("y", DP, None),
        P(DP, "y"),
    )
    return jax.shard_map(
        on_device,
        mesh=cube,
        in_specs=placed,
        out_specs=(
            P(DP, "y"),
            P("y", DP, None),
            P("y", DP, None),
            P("y", DP, None),
        ),
        check_vma=False,
    )
```

```python
import functools

import jax
import jax.numpy as jnp
from jax import lax
from jax.experimental import pallas as pl
from jax.experimental.pallas import tpu as pltpu
from jax.sharding import Mesh
from jax.sharding import PartitionSpec as P

beta_one = 0.9
beta_two = 0.999
adam_step = 10.0
learning_rate = 0.02
epsilon = 1e-08

F32 = jnp.float32
BF16 = jnp.bfloat16
DP = ("z", "x", "c")
MIB = 1 << 20


def two_terms(value):
    high = value.astype(BF16)
    low = (value - high.astype(F32)).astype(BF16)
    return high, low


def dot(a, b):
    return jnp.dot(a, b, preferred_element_type=F32)


def dot_t(a, b, dims):
    return lax.dot_general(a, b, (dims, ((), ())), preferred_element_type=F32)


def project_kernel(core_ref, grad_ref, basis_ref, acts_ref, keep_ref, give_ref, total):
    step = pl.program_id(0)
    high, low = two_terms(basis_ref[...])
    grad = grad_ref[...]
    term = dot(grad, high) + dot(grad, low)

    @pl.when(step == 0)
    def _():
        total[...] = term

    @pl.when(step > 0)
    def _():
        total[...] += term

    @pl.when(step == pl.num_programs(0) - 1)
    def _():
        high, low = two_terms(total[...])
        acts = acts_ref[...]
        term = dot_t(acts, high, ((0,), (0,))) + dot_t(acts, low, ((0,), (0,)))
        term = term.reshape(16, 2, 64, term.shape[-1])
        mine = core_ref[0] == 0
        keep_ref[...] = jnp.where(mine, term[:, 0], term[:, 1])
        give_ref[...] = jnp.where(mine, term[:, 1], term[:, 0]).astype(BF16)


def project(core, acts, out_grad, basis):
    steps = 8
    tokens, width = out_grad.shape
    rank = basis.shape[1]
    depth = width // steps
    return pl.pallas_call(
        project_kernel,
        grid_spec=pltpu.PrefetchScalarGridSpec(
            num_scalar_prefetch=1,
            grid=(steps,),
            in_specs=[
                pl.BlockSpec((tokens, depth), lambda i, core: (0, i)),
                pl.BlockSpec((depth, rank), lambda i, core: (i, 0)),
                pl.BlockSpec(acts.shape, lambda i, core: (0, 0)),
            ],
            out_specs=[pl.BlockSpec((16, 64, rank), lambda i, core: (0, 0, 0))] * 2,
            scratch_shapes=[pltpu.VMEM((tokens, rank), F32)],
        ),
        out_shape=[
            jax.ShapeDtypeStruct((16, 64, rank), F32),
            jax.ShapeDtypeStruct((16, 64, rank), BF16),
        ],
        compiler_params=pltpu.CompilerParams(vmem_limit_bytes=48 * MIB),
        name="project",
    )(core, out_grad, basis, acts)


ORDER = (2, 1, 3, 0)


def exchange_order_kernel(order, y_ref, weight_ref, out_ref):
    for i, d in enumerate(order):
        j = lax.rem(y_ref[0] + d, 4)
        for k in range(8):
            column = pl.multiple_of((j * 8 + k) * 256, 256)
            out_ref[k, :, i * 256 : (i + 1) * 256] = weight_ref[:, pl.ds(column, 256)]


def exchange_order(order, y, weight):
    rows = weight.shape[0]
    return pl.pallas_call(
        functools.partial(exchange_order_kernel, order),
        in_specs=[pl.BlockSpec(memory_space=pltpu.SMEM), pl.BlockSpec(memory_space=pltpu.VMEM)],
        out_shape=jax.ShapeDtypeStruct((8, rows, 256 * len(order)), BF16),
        compiler_params=pltpu.CompilerParams(vmem_limit_bytes=16 * MIB),
        name="exchange_order",
    )(y, weight)


def fresh_kernel(direction_ref, basis_ref, weight_ref, out_ref):
    dh, dl = two_terms(direction_ref[...])
    both = dot_t(jnp.concatenate([dh, dl], axis=0), basis_ref[...].astype(BF16), ((1,), (1,)))
    change = both[: dh.shape[0]] + both[dh.shape[0] :]
    out_ref[...] = (weight_ref[...].astype(F32) - learning_rate * change).astype(BF16)


def fresh_rows(direction, basis, weight):
    rows, width = weight.shape
    block = 2048
    return pl.pallas_call(
        fresh_kernel,
        grid=(width // block,),
        in_specs=[
            pl.BlockSpec(direction.shape, lambda i: (0, 0)),
            pl.BlockSpec((block, basis.shape[1]), lambda i: (i, 0)),
            pl.BlockSpec((rows, block), lambda i: (0, i)),
        ],
        out_specs=pl.BlockSpec((rows, block), lambda i: (0, i)),
        out_shape=jax.ShapeDtypeStruct((rows, width), BF16),
        compiler_params=pltpu.CompilerParams(vmem_limit_bytes=48 * MIB),
        name="fresh_rows",
    )(direction, basis, weight)


def parts_kernel(place_ref, *refs):
    pieces, acts, outs = refs[:5], refs[5:15], refs[15:23]
    rows, tokens, made, row_sems, token_sems, made_sems = refs[23:]
    depth, size = pieces[0].shape[0], tokens.shape[1]
    half = size // 2

    loads = []
    for n, (index, shift) in enumerate(((0, 0), (1, 0), (2, 0), (3, 0), (3, depth // 2))):
        count = pieces[n].shape[0]
        at = pl.ds(pl.multiple_of(place_ref[index] * depth + shift, count), count)
        loads.append(pltpu.make_async_copy(pieces[n], rows.at[at, :], row_sems.at[n]))
    token_loads = []
    for n in range(8):
        h, k = n // 4, n % 4
        copies = []
        for m in range(2):
            source = acts[5 * h + k].at[m * half : (m + 1) * half, :] if k < 3 else acts[5 * h + 3 + m]
            target = tokens.at[n, m * half : (m + 1) * half, :]
            copies.append(pltpu.make_async_copy(source, target, token_sems.at[n, m]))
        token_loads.append(copies)

    for copy in loads + token_loads[0]:
        copy.start()
    for copy in loads:
        copy.wait()

    def store(n, i, h):
        return pltpu.make_async_copy(made.at[n, i], outs[2 * i + h].at[lax.rem(n, 4)], made_sems.at[n, i])

    def body(n, carry):
        for k in range(1, 8):

            @pl.when(n == k - 1)
            def _(k=k):
                for copy in token_loads[k]:
                    copy.start()

        for m in range(2):
            held = tokens.at[n, m * half : (m + 1) * half, :]
            pltpu.make_async_copy(held, held, token_sems.at[n, m]).wait()
        part = dot(tokens[n], rows[...]).astype(BF16)
        for i in range(4):
            made[n, i] = part[:, i * 256 : (i + 1) * 256]
        for h in range(2):

            @pl.when(n // 4 == h)
            def _(h=h):
                for i in range(4):
                    store(n, i, h).start()

        return carry

    lax.fori_loop(0, 8, body, 0)
    for n in range(8):
        for i in range(4):
            store(n, i, n // 4).wait()


def parts(place, pieces, acts):
    tokens, depth = acts[0].shape
    columns = pieces[0].shape[1]
    whole = pl.BlockSpec(memory_space=pl.ANY)
    return pl.pallas_call(
        parts_kernel,
        in_specs=[pl.BlockSpec(memory_space=pltpu.SMEM)] + [whole] * 15,
        out_specs=[whole] * 8,
        scratch_shapes=[
            pltpu.VMEM((depth, columns), BF16),
            pltpu.VMEM((8, tokens, depth), BF16),
            pltpu.VMEM((8, 4, tokens, columns // 4), BF16),
            pltpu.SemaphoreType.DMA((5,)),
            pltpu.SemaphoreType.DMA((8, 2)),
            pltpu.SemaphoreType.DMA((8, 4)),
        ],
        out_shape=[jax.ShapeDtypeStruct((4, tokens, columns // 4), BF16)] * 8,
        compiler_params=pltpu.CompilerParams(vmem_limit_bytes=58 * MIB),
        name="parts",
    )(place, *pieces, *acts)


def sums_kernel(groups, terms, placed, *refs):
    place_ref, refs = (refs[0], refs[1:]) if placed else (None, refs)
    ins, outs = refs[: groups * terms], refs[groups * terms : -4]
    held, made, in_sems, out_sems = refs[-4:]
    loads = [pltpu.make_async_copy(ins[k], held.at[k], in_sems.at[k]) for k in range(groups * terms)]
    for copy in loads:
        copy.start()
    stores = []
    for g in range(groups):
        for k in range(terms):
            loads[g * terms + k].wait()
        for n in range(4):
            total = held[g * terms, n].astype(F32)
            for k in range(1, terms):
                total += held[g * terms + k, n].astype(F32)
            made[g, n] = total.astype(BF16)
            target = outs[0].at[place_ref[4 + 4 * g + n]] if placed else outs[g].at[n]
            stores.append(pltpu.make_async_copy(made.at[g, n], target, out_sems.at[g, n]))
            stores[-1].start()
    for copy in stores:
        copy.wait()


def sums(groups, place=None):
    count, terms, block = len(groups), len(groups[0]), groups[0][0].shape
    whole = pl.BlockSpec(memory_space=pl.ANY)
    placed = place is not None
    shape = jax.ShapeDtypeStruct((4 * count, *block[1:]) if placed else block, BF16)
    return pl.pallas_call(
        functools.partial(sums_kernel, count, terms, placed),
        in_specs=[pl.BlockSpec(memory_space=pltpu.SMEM)] * placed + [whole] * (count * terms),
        out_specs=whole if placed else [whole] * count,
        out_shape=shape if placed else [shape] * count,
        scratch_shapes=[
            pltpu.VMEM((count * terms, *block), BF16),
            pltpu.VMEM((count, *block), BF16),
            pltpu.SemaphoreType.DMA((count * terms,)),
            pltpu.SemaphoreType.DMA((count, 4)),
        ],
        compiler_params=pltpu.CompilerParams(vmem_limit_bytes=58 * MIB),
        name="sums",
    )(*[place] * placed, *[v for g in groups for v in g])


def inner_kernel(core_ref, acts_ref, mine_ref, other_ref, out_ref, rows):
    for k in range(16):
        for ref, core in ((mine_ref, core_ref[0]), (other_ref, 1 - core_ref[0])):
            at = pl.ds(pl.multiple_of(k * 128 + core * 64, 64), 64)
            rows[at, :] = ref[k]
    out_ref[...] = dot(acts_ref[...], rows[...])


def inner(core, acts, mine, other):
    rank = mine.shape[-1]
    whole = lambda a: pl.BlockSpec(a.shape, lambda i, core: (0,) * len(a.shape))
    return pl.pallas_call(
        inner_kernel,
        grid_spec=pltpu.PrefetchScalarGridSpec(
            num_scalar_prefetch=1,
            grid=(1,),
            in_specs=[whole(acts), whole(mine), whole(other)],
            out_specs=pl.BlockSpec((acts.shape[0], rank), lambda i, core: (0, 0)),
            scratch_shapes=[pltpu.VMEM((acts.shape[1], rank), BF16)],
        ),
        out_shape=jax.ShapeDtypeStruct((acts.shape[0], rank), F32),
        compiler_params=pltpu.CompilerParams(vmem_limit_bytes=40 * MIB),
        name="inner",
    )(core, acts, mine, other)


def change_kernel(y_ref, *refs):
    shares, basis_ref, out_ref = refs[:4], refs[4], refs[5]
    total = shares[0][...].astype(F32)
    for ref in shares[1:]:
        total += ref[...].astype(F32)
    zh, zl = two_terms(total)
    both = dot_t(jnp.concatenate([zh, zl], axis=0), basis_ref[...].astype(BF16), ((1,), (1,)))
    out_ref[...] = (learning_rate * (both[: zh.shape[0]] + both[zh.shape[0] :])).astype(BF16)


def change_of(y, shares, basis):
    columns = 1024
    tokens, rank = shares[0].shape
    return pl.pallas_call(
        change_kernel,
        grid_spec=pltpu.PrefetchScalarGridSpec(
            num_scalar_prefetch=1,
            grid=(2,),
            in_specs=[pl.BlockSpec((tokens, rank), lambda i, y: (0, 0))] * 4
            + [pl.BlockSpec((columns, rank), lambda i, y: (y[0] * 2 + i, 0))],
            out_specs=pl.BlockSpec((tokens, columns), lambda i, y: (0, i)),
        ),
        out_shape=jax.ShapeDtypeStruct((tokens, 2 * columns), BF16),
        compiler_params=pltpu.CompilerParams(vmem_limit_bytes=24 * MIB),
        name="change",
    )(y, *shares, basis)


def halves_kernel(first_ref, last_ref, *out_refs):
    out_refs[0][...] = first_ref[...]
    out_refs[1][...] = last_ref[...]


def halves(first, last):
    rows, width = first.shape
    shape = (rows // 2, width)
    return pl.pallas_call(
        halves_kernel,
        grid=(1,),
        in_specs=[pl.BlockSpec(shape, lambda i: (0, 0)), pl.BlockSpec(shape, lambda i: (1, 0))],
        out_specs=[pl.BlockSpec(shape, lambda i: (0, 0))] * 2,
        out_shape=[jax.ShapeDtypeStruct(shape, BF16)] * 2,
        compiler_params=pltpu.CompilerParams(vmem_limit_bytes=16 * MIB),
        name="halves",
    )(first, last)


def output_kernel(part_ref, change_ref, out_ref):
    for n in range(part_ref.shape[0]):
        columns = slice(n * 256, (n + 1) * 256)
        total = part_ref[n].astype(F32) - change_ref[:, columns].astype(F32)
        out_ref[:, columns] = total.astype(BF16)


def output_rows(part, change):
    blocks, tokens, columns = part.shape
    return pl.pallas_call(
        output_kernel,
        grid=(2,),
        in_specs=[
            pl.BlockSpec((blocks // 2, tokens, columns), lambda i: (i, 0, 0)),
            pl.BlockSpec((tokens, blocks // 2 * columns), lambda i: (0, i)),
        ],
        out_specs=pl.BlockSpec((tokens, blocks // 2 * columns), lambda i: (0, i)),
        out_shape=jax.ShapeDtypeStruct((tokens, blocks * columns), BF16),
        name="output_rows",
    )(part, change)


def swap(value):
    return lax.ppermute(value, "c", [(0, 1), (1, 0)])


def shift(value, axis, by):
    return lax.ppermute(value, axis, [(i, (i + by) % 4) for i in range(4)])


def on_device(acts, out_grad, basis, moment1, moment2, weight, next_acts):
    z, x, c, y = (lax.axis_index(a).astype(jnp.int32) for a in ("z", "x", "c", "y"))
    core, tensor = c[None], y[None]
    old = weight[0]
    keep, give = project(core, acts, out_grad, basis)
    own = lax.all_to_all(exchange_order(ORDER, tensor, old), ("x", "c"), 0, 0)
    got, beside = swap(give), swap(next_acts)
    own, keep, got, tokens, beside = lax.optimization_barrier((own, keep, got, next_acts, beside))
    own = own.reshape(512, 1024)
    near = (shift(own, "z", 1), shift(own, "z", -1), shift(tokens, "x", 1), shift(tokens, "x", -1))
    right, left, tr, tl = lax.optimization_barrier(near)
    ta, tb = halves(tr, tl)
    ta, tb, right, left = lax.optimization_barrier((ta, tb, right, left))
    near_a, near_b = halves(right, left)
    ta, tb = shift(ta, "x", 1), shift(tb, "x", -1)
    far_a, far_b = shift(near_a, "z", 1), shift(near_b, "z", -1)
    ta, tb, tr, tl, far_a, far_b = lax.optimization_barrier((ta, tb, tr, tl, far_a, far_b))
    pieces = (own, right, left, far_a, far_b)
    blocks = (tokens, tr, tl, ta, tb)
    others = (beside, *(swap(v) for v in blocks[1:]))
    place = [(v + d) % 4 for v in (z, x) for d in (0, 3, 1, 2)]
    place = jnp.stack(place[:4] + [2 * v + c for v in place[4:]] + [2 * v + 1 - c for v in place[4:]])
    up2, down2, up1, down1, up3, down3, up0, down0 = parts(place, pieces, blocks + others)
    got_up2, got_down2 = shift(up2, "y", 1), shift(down2, "y", -1)
    keep, got, up2 = lax.optimization_barrier((keep, got, up2))
    projected = (keep + got.astype(F32)).astype(BF16)
    projected = lax.all_to_all(projected, ("z", "x"), 0, 0)
    got_down1, got_up3 = shift(down1, "y", 1), shift(up3, "y", -1)
    up1, down3 = sums(((up1, got_up2), (down3, got_down2)))
    got_up1, got_down3 = shift(up1, "y", 1), shift(down3, "y", -1)
    projected, up1 = lax.optimization_barrier((projected, up1))
    projected = jnp.sum(projected.astype(F32), axis=0)
    first = beta_one * moment1[0] + (1.0 - beta_one) * projected
    second = beta_two * moment2[0] + (1.0 - beta_two) * projected * projected
    direction = (
        first
        / (1.0 - beta_one**adam_step)
        / (jnp.sqrt(second / (1.0 - beta_two**adam_step)) + epsilon)
    )
    sent = jnp.broadcast_to(direction.astype(BF16)[None], (16, 64, 256))
    mine = lax.all_to_all(sent, ("z", "x"), 0, 0)
    fresh = fresh_rows(direction, basis, old)
    up0, down0, fresh, mine = lax.optimization_barrier((up0, down0, fresh, mine))
    part = sums(((up0, got_up1, got_up3), (down0, got_down1, got_down3)), place)
    part, mine = lax.optimization_barrier((part, mine))
    share = inner(core, next_acts, mine, swap(mine)).astype(BF16)
    shares = [share] + [shift(share, "y", d) for d in (1, -1, 2)]
    change = change_of(tensor, shares, basis)
    part = lax.all_to_all(part, ("x", "c"), 0, 0)
    output = output_rows(part, change)
    return (output, fresh[None], first[None], second[None])


def solution(mesh):
    cube = Mesh(mesh.devices.reshape(4, 4, 2, 4), ("z", "x", "c", "y"))
    placed = (
        P(DP, "y"),
        P(DP, None),
        P(),
        P("y", DP, None),
        P("y", DP, None),
        P("y", DP, None),
        P(DP, "y"),
    )
    return jax.shard_map(
        on_device,
        mesh=cube,
        in_specs=placed,
        out_specs=(
            P(DP, "y"),
            P("y", DP, None),
            P("y", DP, None),
            P("y", DP, None),
        ),
        check_vma=False,
    )
```

```python
import functools

import jax
import jax.numpy as jnp
from jax import lax
from jax.experimental import pallas as pl
from jax.experimental.pallas import tpu as pltpu
from jax.sharding import Mesh
from jax.sharding import PartitionSpec as P

beta_one = 0.9
beta_two = 0.999
adam_step = 10.0
learning_rate = 0.02
epsilon = 1e-08

F32 = jnp.float32
BF16 = jnp.bfloat16
DP = ("z", "x", "c")
MIB = 1 << 20


def two_terms(value):
    high = value.astype(BF16)
    low = (value - high.astype(F32)).astype(BF16)
    return high, low


def dot(a, b):
    return jnp.dot(a, b, preferred_element_type=F32)


def dot_t(a, b, dims):
    return lax.dot_general(a, b, (dims, ((), ())), preferred_element_type=F32)


def project_kernel(core_ref, grad_ref, basis_ref, acts_ref, keep_ref, give_ref, total):
    step = pl.program_id(0)
    high, low = two_terms(basis_ref[...])
    grad = grad_ref[...]
    term = dot(grad, high) + dot(grad, low)

    @pl.when(step == 0)
    def _():
        total[...] = term

    @pl.when(step > 0)
    def _():
        total[...] += term

    @pl.when(step == pl.num_programs(0) - 1)
    def _():
        high, low = two_terms(total[...])
        acts = acts_ref[...]
        term = dot_t(acts, high, ((0,), (0,))) + dot_t(acts, low, ((0,), (0,)))
        term = term.reshape(16, 2, 64, term.shape[-1])
        mine = core_ref[0] == 0
        keep_ref[...] = jnp.where(mine, term[:, 0], term[:, 1])
        give_ref[...] = jnp.where(mine, term[:, 1], term[:, 0]).astype(BF16)


def project(core, acts, out_grad, basis):
    steps = 8
    tokens, width = out_grad.shape
    rank = basis.shape[1]
    depth = width // steps
    return pl.pallas_call(
        project_kernel,
        grid_spec=pltpu.PrefetchScalarGridSpec(
            num_scalar_prefetch=1,
            grid=(steps,),
            in_specs=[
                pl.BlockSpec((tokens, depth), lambda i, core: (0, i)),
                pl.BlockSpec((depth, rank), lambda i, core: (i, 0)),
                pl.BlockSpec(acts.shape, lambda i, core: (0, 0)),
            ],
            out_specs=[pl.BlockSpec((16, 64, rank), lambda i, core: (0, 0, 0))] * 2,
            scratch_shapes=[pltpu.VMEM((tokens, rank), F32)],
        ),
        out_shape=[
            jax.ShapeDtypeStruct((16, 64, rank), F32),
            jax.ShapeDtypeStruct((16, 64, rank), BF16),
        ],
        compiler_params=pltpu.CompilerParams(vmem_limit_bytes=48 * MIB),
        name="project",
    )(core, out_grad, basis, acts)


ORDER = (2, 1, 3, 0)


def exchange_order_kernel(order, y_ref, weight_ref, out_ref, held, sems):
    loads = []
    for i, d in enumerate(order):
        column = pl.multiple_of(lax.rem(y_ref[0] + d, 4) * 2048, 2048)
        loads.append(pltpu.make_async_copy(weight_ref.at[:, pl.ds(column, 2048)], held.at[i], sems.at[i]))
    for copy in loads:
        copy.start()
    for i, copy in enumerate(loads):
        copy.wait()
        for k in range(8):
            out_ref[k, :, i * 256 : (i + 1) * 256] = held[i, :, k * 256 : (k + 1) * 256]


def exchange_order(order, y, weight):
    rows = weight.shape[0]
    count = len(order)
    return pl.pallas_call(
        functools.partial(exchange_order_kernel, order),
        in_specs=[pl.BlockSpec(memory_space=pltpu.SMEM), pl.BlockSpec(memory_space=pl.ANY)],
        out_shape=jax.ShapeDtypeStruct((8, rows, 256 * count), BF16),
        scratch_shapes=[pltpu.VMEM((count, rows, 2048), BF16), pltpu.SemaphoreType.DMA((count,))],
        compiler_params=pltpu.CompilerParams(vmem_limit_bytes=58 * MIB),
        name="exchange_order",
    )(y, weight)


def fresh_kernel(direction_ref, basis_ref, weight_ref, out_ref):
    dh, dl = two_terms(direction_ref[...])
    both = dot_t(jnp.concatenate([dh, dl], axis=0), basis_ref[...].astype(BF16), ((1,), (1,)))
    change = both[: dh.shape[0]] + both[dh.shape[0] :]
    out_ref[...] = (weight_ref[...].astype(F32) - learning_rate * change).astype(BF16)


def fresh_rows(direction, basis, weight):
    rows, width = weight.shape
    block = 2048
    return pl.pallas_call(
        fresh_kernel,
        grid=(width // block,),
        in_specs=[
            pl.BlockSpec(direction.shape, lambda i: (0, 0)),
            pl.BlockSpec((block, basis.shape[1]), lambda i: (i, 0)),
            pl.BlockSpec((rows, block), lambda i: (0, i)),
        ],
        out_specs=pl.BlockSpec((rows, block), lambda i: (0, i)),
        out_shape=jax.ShapeDtypeStruct((rows, width), BF16),
        compiler_params=pltpu.CompilerParams(vmem_limit_bytes=48 * MIB),
        name="fresh_rows",
    )(direction, basis, weight)


def parts_kernel(place_ref, *refs):
    pieces, acts, outs = refs[:5], refs[5:15], refs[15:23]
    rows, tokens, made, row_sems, token_sems, made_sems = refs[23:]
    depth, size = pieces[0].shape[0], tokens.shape[1]
    half = size // 2

    loads = []
    for n, (index, shift) in enumerate(((0, 0), (1, 0), (2, 0), (3, 0), (3, depth // 2))):
        count = pieces[n].shape[0]
        at = pl.ds(pl.multiple_of(place_ref[index] * depth + shift, count), count)
        loads.append(pltpu.make_async_copy(pieces[n], rows.at[at, :], row_sems.at[n]))
    token_loads = []
    for n in range(8):
        h, k = n // 4, n % 4
        copies = []
        for m in range(2):
            source = acts[5 * h + k].at[m * half : (m + 1) * half, :] if k < 3 else acts[5 * h + 3 + m]
            target = tokens.at[n, m * half : (m + 1) * half, :]
            copies.append(pltpu.make_async_copy(source, target, token_sems.at[n, m]))
        token_loads.append(copies)

    for copy in loads + token_loads[0]:
        copy.start()
    for copy in loads:
        copy.wait()

    def store(n, i, h):
        return pltpu.make_async_copy(made.at[n, i], outs[2 * i + h].at[lax.rem(n, 4)], made_sems.at[n, i])

    def body(n, carry):
        for k in range(1, 8):

            @pl.when(n == k - 1)
            def _(k=k):
                for copy in token_loads[k]:
                    copy.start()

        for m in range(2):
            held = tokens.at[n, m * half : (m + 1) * half, :]
            pltpu.make_async_copy(held, held, token_sems.at[n, m]).wait()
        part = dot(tokens[n], rows[...]).astype(BF16)
        for i in range(4):
            made[n, i] = part[:, i * 256 : (i + 1) * 256]
        for h in range(2):

            @pl.when(n // 4 == h)
            def _(h=h):
                for i in range(4):
                    store(n, i, h).start()

        return carry

    lax.fori_loop(0, 8, body, 0)
    for n in range(8):
        for i in range(4):
            store(n, i, n // 4).wait()


def parts(place, pieces, acts):
    tokens, depth = acts[0].shape
    columns = pieces[0].shape[1]
    whole = pl.BlockSpec(memory_space=pl.ANY)
    return pl.pallas_call(
        parts_kernel,
        in_specs=[pl.BlockSpec(memory_space=pltpu.SMEM)] + [whole] * 15,
        out_specs=[whole] * 8,
        scratch_shapes=[
            pltpu.VMEM((depth, columns), BF16),
            pltpu.VMEM((8, tokens, depth), BF16),
            pltpu.VMEM((8, 4, tokens, columns // 4), BF16),
            pltpu.SemaphoreType.DMA((5,)),
            pltpu.SemaphoreType.DMA((8, 2)),
            pltpu.SemaphoreType.DMA((8, 4)),
        ],
        out_shape=[jax.ShapeDtypeStruct((4, tokens, columns // 4), BF16)] * 8,
        compiler_params=pltpu.CompilerParams(vmem_limit_bytes=58 * MIB),
        name="parts",
    )(place, *pieces, *acts)


def sums_kernel(groups, terms, placed, *refs):
    place_ref, refs = (refs[0], refs[1:]) if placed else (None, refs)
    ins, outs = refs[: groups * terms], refs[groups * terms : -4]
    held, made, in_sems, out_sems = refs[-4:]
    loads = [pltpu.make_async_copy(ins[k], held.at[k], in_sems.at[k]) for k in range(groups * terms)]
    for copy in loads:
        copy.start()
    stores = []
    for g in range(groups):
        for k in range(terms):
            loads[g * terms + k].wait()
        for n in range(4):
            total = held[g * terms, n].astype(F32)
            for k in range(1, terms):
                total += held[g * terms + k, n].astype(F32)
            made[g, n] = total.astype(BF16)
            target = outs[0].at[place_ref[4 + 4 * g + n]] if placed else outs[g].at[n]
            stores.append(pltpu.make_async_copy(made.at[g, n], target, out_sems.at[g, n]))
            stores[-1].start()
    for copy in stores:
        copy.wait()


def sums(groups, place=None):
    count, terms, block = len(groups), len(groups[0]), groups[0][0].shape
    whole = pl.BlockSpec(memory_space=pl.ANY)
    placed = place is not None
    shape = jax.ShapeDtypeStruct((4 * count, *block[1:]) if placed else block, BF16)
    return pl.pallas_call(
        functools.partial(sums_kernel, count, terms, placed),
        in_specs=[pl.BlockSpec(memory_space=pltpu.SMEM)] * placed + [whole] * (count * terms),
        out_specs=whole if placed else [whole] * count,
        out_shape=shape if placed else [shape] * count,
        scratch_shapes=[
            pltpu.VMEM((count * terms, *block), BF16),
            pltpu.VMEM((count, *block), BF16),
            pltpu.SemaphoreType.DMA((count * terms,)),
            pltpu.SemaphoreType.DMA((count, 4)),
        ],
        compiler_params=pltpu.CompilerParams(vmem_limit_bytes=58 * MIB),
        name="sums",
    )(*[place] * placed, *[v for g in groups for v in g])


def inner_kernel(core_ref, acts_ref, mine_ref, other_ref, out_ref, rows):
    for k in range(16):
        for ref, core in ((mine_ref, core_ref[0]), (other_ref, 1 - core_ref[0])):
            at = pl.ds(pl.multiple_of(k * 128 + core * 64, 64), 64)
            rows[at, :] = ref[k]
    out_ref[...] = dot(acts_ref[...], rows[...])


def inner(core, acts, mine, other):
    rank = mine.shape[-1]
    whole = lambda a: pl.BlockSpec(a.shape, lambda i, core: (0,) * len(a.shape))
    return pl.pallas_call(
        inner_kernel,
        grid_spec=pltpu.PrefetchScalarGridSpec(
            num_scalar_prefetch=1,
            grid=(1,),
            in_specs=[whole(acts), whole(mine), whole(other)],
            out_specs=pl.BlockSpec((acts.shape[0], rank), lambda i, core: (0, 0)),
            scratch_shapes=[pltpu.VMEM((acts.shape[1], rank), BF16)],
        ),
        out_shape=jax.ShapeDtypeStruct((acts.shape[0], rank), F32),
        compiler_params=pltpu.CompilerParams(vmem_limit_bytes=40 * MIB),
        name="inner",
    )(core, acts, mine, other)


def change_kernel(*refs):
    shares, basis_ref, out_ref = refs[:4], refs[4], refs[5]
    total = shares[0][...].astype(F32)
    for ref in shares[1:]:
        total += ref[...].astype(F32)
    zh, zl = two_terms(total)
    both = dot_t(jnp.concatenate([zh, zl], axis=0), basis_ref[...], ((1,), (1,)))
    out_ref[...] = (learning_rate * (both[: zh.shape[0]] + both[zh.shape[0] :])).astype(BF16)


def change_of(shares, basis):
    columns = 1024
    tokens, rank = shares[0].shape
    return pl.pallas_call(
        change_kernel,
        grid=(2,),
        in_specs=[pl.BlockSpec((tokens, rank), lambda i: (0, 0))] * 4
        + [pl.BlockSpec((columns, rank), lambda i: (i, 0))],
        out_specs=pl.BlockSpec((tokens, columns), lambda i: (0, i)),
        out_shape=jax.ShapeDtypeStruct((tokens, 2 * columns), BF16),
        compiler_params=pltpu.CompilerParams(vmem_limit_bytes=24 * MIB),
        name="change",
    )(*shares, basis)


def halves_kernel(first_ref, last_ref, *out_refs):
    out_refs[0][...] = first_ref[...]
    out_refs[1][...] = last_ref[...]


def halves(first, last):
    rows, width = first.shape
    shape = (rows // 2, width)
    return pl.pallas_call(
        halves_kernel,
        grid=(1,),
        in_specs=[pl.BlockSpec(shape, lambda i: (0, 0)), pl.BlockSpec(shape, lambda i: (1, 0))],
        out_specs=[pl.BlockSpec(shape, lambda i: (0, 0))] * 2,
        out_shape=[jax.ShapeDtypeStruct(shape, BF16)] * 2,
        compiler_params=pltpu.CompilerParams(vmem_limit_bytes=16 * MIB),
        name="halves",
    )(first, last)


def output_kernel(part_ref, change_ref, out_ref):
    for n in range(part_ref.shape[0]):
        columns = slice(n * 256, (n + 1) * 256)
        total = part_ref[n].astype(F32) - change_ref[:, columns].astype(F32)
        out_ref[:, columns] = total.astype(BF16)


def output_rows(part, change):
    blocks, tokens, columns = part.shape
    return pl.pallas_call(
        output_kernel,
        grid=(2,),
        in_specs=[
            pl.BlockSpec((blocks // 2, tokens, columns), lambda i: (i, 0, 0)),
            pl.BlockSpec((tokens, blocks // 2 * columns), lambda i: (0, i)),
        ],
        out_specs=pl.BlockSpec((tokens, blocks // 2 * columns), lambda i: (0, i)),
        out_shape=jax.ShapeDtypeStruct((tokens, blocks * columns), BF16),
        compiler_params=pltpu.CompilerParams(vmem_limit_bytes=24 * MIB),
        name="output_rows",
    )(part, change)


def swap(value):
    return lax.ppermute(value, "c", [(0, 1), (1, 0)])


def shift(value, axis, by):
    return lax.ppermute(value, axis, [(i, (i + by) % 4) for i in range(4)])


def on_device(acts, out_grad, basis, moment1, moment2, weight, next_acts):
    z, x, c, y = (lax.axis_index(a).astype(jnp.int32) for a in ("z", "x", "c", "y"))
    core, tensor = c[None], y[None]
    old = weight[0]
    keep, give = project(core, acts, out_grad, basis)
    own = lax.all_to_all(exchange_order(ORDER, tensor, old), ("x", "c"), 0, 0)
    got, beside = swap(give), swap(next_acts)
    rows = lax.dynamic_slice_in_dim(basis, y * 2048, 2048, axis=0).astype(BF16)
    own, keep, got, tokens, beside, rows = lax.optimization_barrier((own, keep, got, next_acts, beside, rows))
    own = own.reshape(512, 1024)
    near = (shift(own, "z", 1), shift(own, "z", -1), shift(tokens, "x", 1), shift(tokens, "x", -1))
    right, left, tr, tl = lax.optimization_barrier(near)
    ta, tb = halves(tr, tl)
    ta, tb, right, left = lax.optimization_barrier((ta, tb, right, left))
    near_a, near_b = halves(right, left)
    ta, tb = shift(ta, "x", 1), shift(tb, "x", -1)
    far_a, far_b = shift(near_a, "z", 1), shift(near_b, "z", -1)
    ta, tb, tr, tl, far_a, far_b = lax.optimization_barrier((ta, tb, tr, tl, far_a, far_b))
    pieces = (own, right, left, far_a, far_b)
    blocks = (tokens, tr, tl, ta, tb)
    others = (beside, *(swap(v) for v in blocks[1:]))
    place = [(v + d) % 4 for v in (z, x) for d in (0, 3, 1, 2)]
    place = jnp.stack(place[:4] + [2 * v + c for v in place[4:]] + [2 * v + 1 - c for v in place[4:]])
    up2, down2, up1, down1, up3, down3, up0, down0 = parts(place, pieces, blocks + others)
    got_up2, got_down2 = shift(up2, "y", 1), shift(down2, "y", -1)
    keep, got, up2 = lax.optimization_barrier((keep, got, up2))
    projected = (keep + got.astype(F32)).astype(BF16)
    projected = lax.all_to_all(projected, ("z", "x"), 0, 0)
    got_down1, got_up3 = shift(down1, "y", 1), shift(up3, "y", -1)
    up1, down3 = sums(((up1, got_up2), (down3, got_down2)))
    got_up1, got_down3 = shift(up1, "y", 1), shift(down3, "y", -1)
    projected, up1 = lax.optimization_barrier((projected, up1))
    projected = jnp.sum(projected.astype(F32), axis=0)
    first = beta_one * moment1[0] + (1.0 - beta_one) * projected
    second = beta_two * moment2[0] + (1.0 - beta_two) * projected * projected
    direction = (
        first
        / (1.0 - beta_one**adam_step)
        / (jnp.sqrt(second / (1.0 - beta_two**adam_step)) + epsilon)
    )
    sent = jnp.broadcast_to(direction.astype(BF16)[None], (16, 64, 256))
    mine = lax.all_to_all(sent, ("z", "x"), 0, 0)
    fresh = fresh_rows(direction, basis, old)
    up0, down0, fresh = lax.optimization_barrier((up0, down0, fresh))
    part = sums(((up0, got_up1, got_up3), (down0, got_down1, got_down3)), place)
    part, mine = lax.optimization_barrier((part, mine))
    share = inner(core, next_acts, mine, swap(mine)).astype(BF16)
    shares = [share] + [shift(share, "y", d) for d in (1, -1, 2)]
    change = change_of(shares, rows)
    part = lax.all_to_all(part, ("x", "c"), 0, 0)
    output = output_rows(part, change)
    return (output, fresh[None], first[None], second[None])


def solution(mesh):
    cube = Mesh(mesh.devices.reshape(4, 4, 2, 4), ("z", "x", "c", "y"))
    placed = (
        P(DP, "y"),
        P(DP, None),
        P(),
        P("y", DP, None),
        P("y", DP, None),
        P("y", DP, None),
        P(DP, "y"),
    )
    return jax.shard_map(
        on_device,
        mesh=cube,
        in_specs=placed,
        out_specs=(
            P(DP, "y"),
            P("y", DP, None),
            P("y", DP, None),
            P("y", DP, None),
        ),
        check_vma=False,
    )
```

```python
import functools

import jax
import jax.numpy as jnp
from jax import lax
from jax.experimental import pallas as pl
from jax.experimental.pallas import tpu as pltpu
from jax.sharding import Mesh
from jax.sharding import PartitionSpec as P

beta_one = 0.9
beta_two = 0.999
adam_step = 10.0
learning_rate = 0.02
epsilon = 1e-08

F32 = jnp.float32
BF16 = jnp.bfloat16
DP = ("z", "x", "c")
MIB = 1 << 20


def two_terms(value):
    high = value.astype(BF16)
    low = (value - high.astype(F32)).astype(BF16)
    return high, low


def dot(a, b):
    return jnp.dot(a, b, preferred_element_type=F32)


def dot_t(a, b, dims):
    return lax.dot_general(a, b, (dims, ((), ())), preferred_element_type=F32)


def project_kernel(core_ref, grad_ref, basis_ref, acts_ref, keep_ref, give_ref, total):
    step = pl.program_id(0)
    high, low = two_terms(basis_ref[...])
    grad = grad_ref[...]
    term = dot(grad, high) + dot(grad, low)

    @pl.when(step == 0)
    def _():
        total[...] = term

    @pl.when(step > 0)
    def _():
        total[...] += term

    @pl.when(step == pl.num_programs(0) - 1)
    def _():
        high, low = two_terms(total[...])
        acts = acts_ref[...]
        term = dot_t(acts, high, ((0,), (0,))) + dot_t(acts, low, ((0,), (0,)))
        term = term.reshape(16, 2, 64, term.shape[-1])
        mine = core_ref[0] == 0
        keep_ref[...] = jnp.where(mine, term[:, 0], term[:, 1])
        give_ref[...] = jnp.where(mine, term[:, 1], term[:, 0]).astype(BF16)


def project(core, acts, out_grad, basis):
    steps = 8
    tokens, width = out_grad.shape
    rank = basis.shape[1]
    depth = width // steps
    return pl.pallas_call(
        project_kernel,
        grid_spec=pltpu.PrefetchScalarGridSpec(
            num_scalar_prefetch=1,
            grid=(steps,),
            in_specs=[
                pl.BlockSpec((tokens, depth), lambda i, core: (0, i)),
                pl.BlockSpec((depth, rank), lambda i, core: (i, 0)),
                pl.BlockSpec(acts.shape, lambda i, core: (0, 0)),
            ],
            out_specs=[pl.BlockSpec((16, 64, rank), lambda i, core: (0, 0, 0))] * 2,
            scratch_shapes=[pltpu.VMEM((tokens, rank), F32)],
        ),
        out_shape=[
            jax.ShapeDtypeStruct((16, 64, rank), F32),
            jax.ShapeDtypeStruct((16, 64, rank), BF16),
        ],
        compiler_params=pltpu.CompilerParams(vmem_limit_bytes=48 * MIB),
        name="project",
    )(core, out_grad, basis, acts)


ORDER = (2, 1, 3, 0)


def exchange_order_kernel(order, y_ref, weight_ref, out_ref, held, sems):
    loads = []
    for i, d in enumerate(order):
        column = pl.multiple_of(lax.rem(y_ref[0] + d, 4) * 2048, 2048)
        loads.append(pltpu.make_async_copy(weight_ref.at[:, pl.ds(column, 2048)], held.at[i], sems.at[i]))
    for copy in loads:
        copy.start()
    for i, copy in enumerate(loads):
        copy.wait()
        for k in range(8):
            out_ref[k, :, i * 256 : (i + 1) * 256] = held[i, :, k * 256 : (k + 1) * 256]


def exchange_order(order, y, weight):
    rows = weight.shape[0]
    count = len(order)
    return pl.pallas_call(
        functools.partial(exchange_order_kernel, order),
        in_specs=[pl.BlockSpec(memory_space=pltpu.SMEM), pl.BlockSpec(memory_space=pl.ANY)],
        out_shape=jax.ShapeDtypeStruct((8, rows, 256 * count), BF16),
        scratch_shapes=[pltpu.VMEM((count, rows, 2048), BF16), pltpu.SemaphoreType.DMA((count,))],
        compiler_params=pltpu.CompilerParams(vmem_limit_bytes=58 * MIB),
        name="exchange_order",
    )(y, weight)


def fresh_kernel(direction_ref, basis_ref, weight_ref, out_ref):
    dh, dl = two_terms(direction_ref[...])
    both = dot_t(jnp.concatenate([dh, dl], axis=0), basis_ref[...].astype(BF16), ((1,), (1,)))
    change = both[: dh.shape[0]] + both[dh.shape[0] :]
    out_ref[...] = (weight_ref[...].astype(F32) - learning_rate * change).astype(BF16)


def fresh_rows(direction, basis, weight):
    rows, width = weight.shape
    block = 2048
    return pl.pallas_call(
        fresh_kernel,
        grid=(width // block,),
        in_specs=[
            pl.BlockSpec(direction.shape, lambda i: (0, 0)),
            pl.BlockSpec((block, basis.shape[1]), lambda i: (i, 0)),
            pl.BlockSpec((rows, block), lambda i: (0, i)),
        ],
        out_specs=pl.BlockSpec((rows, block), lambda i: (0, i)),
        out_shape=jax.ShapeDtypeStruct((rows, width), BF16),
        compiler_params=pltpu.CompilerParams(vmem_limit_bytes=48 * MIB),
        name="fresh_rows",
    )(direction, basis, weight)


def parts_kernel(place_ref, *refs):
    pieces, acts, outs = refs[:5], refs[5:10], refs[10:14]
    rows, tokens, made, row_sems, token_sems, made_sems = refs[14:]
    depth, size = pieces[0].shape[0], tokens.shape[1]
    half = size // 2

    loads = []
    for n, (index, shift) in enumerate(((0, 0), (1, 0), (2, 0), (3, 0), (3, depth // 2))):
        count = pieces[n].shape[0]
        at = pl.ds(pl.multiple_of(place_ref[index] * depth + shift, count), count)
        loads.append(pltpu.make_async_copy(pieces[n], rows.at[at, :], row_sems.at[n]))
    token_loads = [[pltpu.make_async_copy(acts[n], tokens.at[n], token_sems.at[n])] for n in range(3)]
    token_loads.append(
        [
            pltpu.make_async_copy(acts[3 + m], tokens.at[3, m * half : (m + 1) * half, :], token_sems.at[3 + m])
            for m in range(2)
        ]
    )
    for copy in loads + token_loads[0]:
        copy.start()
    for copy in loads:
        copy.wait()
    stores = []
    for n in range(4):
        if n < 3:
            for copy in token_loads[n + 1]:
                copy.start()
        for copy in token_loads[n]:
            copy.wait()
        part = dot(tokens[n], rows[...]).astype(BF16)
        for i in range(4):
            made[n, i] = part[:, i * 256 : (i + 1) * 256]
            stores.append(pltpu.make_async_copy(made.at[n, i], outs[i].at[n], made_sems.at[n, i]))
            stores[-1].start()
    for copy in stores:
        copy.wait()


def parts(place, pieces, acts):
    tokens, depth = acts[0].shape
    whole = pl.BlockSpec(memory_space=pl.ANY)
    return pl.pallas_call(
        parts_kernel,
        in_specs=[pl.BlockSpec(memory_space=pltpu.SMEM)] + [whole] * 10,
        out_specs=[whole] * 4,
        scratch_shapes=[
            pltpu.VMEM((depth, pieces[0].shape[1]), BF16),
            pltpu.VMEM((4, tokens, depth), BF16),
            pltpu.VMEM((4, 4, tokens, 256), BF16),
            pltpu.SemaphoreType.DMA((5,)),
            pltpu.SemaphoreType.DMA((5,)),
            pltpu.SemaphoreType.DMA((4, 4)),
        ],
        out_shape=[jax.ShapeDtypeStruct((4, tokens, 256), BF16)] * 4,
        compiler_params=pltpu.CompilerParams(vmem_limit_bytes=58 * MIB),
        name="parts",
    )(place, *pieces, *acts)


def sums_kernel(groups, terms, placed, *refs):
    place_ref, refs = (refs[0], refs[1:]) if placed else (None, refs)
    ins, outs = refs[: groups * terms], refs[groups * terms : -4]
    held, made, in_sems, out_sems = refs[-4:]
    loads = [pltpu.make_async_copy(ins[k], held.at[k], in_sems.at[k]) for k in range(groups * terms)]
    for copy in loads:
        copy.start()
    stores = []
    for g in range(groups):
        for k in range(terms):
            loads[g * terms + k].wait()
        for n in range(4):
            total = held[g * terms, n].astype(F32)
            for k in range(1, terms):
                total += held[g * terms + k, n].astype(F32)
            made[g, n] = total.astype(BF16)
            target = outs[0].at[place_ref[4 + 4 * g + n]] if placed else outs[g].at[n]
            stores.append(pltpu.make_async_copy(made.at[g, n], target, out_sems.at[g, n]))
            stores[-1].start()
    for copy in stores:
        copy.wait()


def sums(groups, place=None):
    count, terms, block = len(groups), len(groups[0]), groups[0][0].shape
    whole = pl.BlockSpec(memory_space=pl.ANY)
    placed = place is not None
    shape = jax.ShapeDtypeStruct((4 * count, *block[1:]) if placed else block, BF16)
    return pl.pallas_call(
        functools.partial(sums_kernel, count, terms, placed),
        in_specs=[pl.BlockSpec(memory_space=pltpu.SMEM)] * placed + [whole] * (count * terms),
        out_specs=whole if placed else [whole] * count,
        out_shape=shape if placed else [shape] * count,
        scratch_shapes=[
            pltpu.VMEM((count * terms, *block), BF16),
            pltpu.VMEM((count, *block), BF16),
            pltpu.SemaphoreType.DMA((count * terms,)),
            pltpu.SemaphoreType.DMA((count, 4)),
        ],
        compiler_params=pltpu.CompilerParams(vmem_limit_bytes=58 * MIB),
        name="sums",
    )(*[place] * placed, *[v for g in groups for v in g])


def step_kernel(terms_ref, one_ref, two_ref, first_ref, second_ref, direction_ref, sent_ref):
    projected = jnp.sum(terms_ref[...].astype(F32), axis=0)
    first = beta_one * one_ref[...] + (1.0 - beta_one) * projected
    second = beta_two * two_ref[...] + (1.0 - beta_two) * projected * projected
    direction = (
        first
        / (1.0 - beta_one**adam_step)
        / (jnp.sqrt(second / (1.0 - beta_two**adam_step)) + epsilon)
    )
    first_ref[...] = first
    second_ref[...] = second
    direction_ref[...] = direction
    sent_ref[...] = jnp.broadcast_to(direction.astype(BF16)[None], sent_ref.shape)


def optimizer_step(terms, one, two):
    shape = jax.ShapeDtypeStruct(one.shape, F32)
    return pl.pallas_call(
        step_kernel,
        out_shape=[shape] * 3 + [jax.ShapeDtypeStruct(terms.shape, BF16)],
        compiler_params=pltpu.CompilerParams(vmem_limit_bytes=16 * MIB),
        name="optimizer_step",
    )(terms, one, two)


def inner_kernel(core_ref, acts_ref, mine_ref, other_ref, out_ref, rows):
    for k in range(16):
        for ref, core in ((mine_ref, core_ref[0]), (other_ref, 1 - core_ref[0])):
            at = pl.ds(pl.multiple_of(k * 128 + core * 64, 64), 64)
            rows[at, :] = ref[k]
    out_ref[...] = dot(acts_ref[...], rows[...])


def inner(core, acts, mine, other):
    rank = mine.shape[-1]
    whole = lambda a: pl.BlockSpec(a.shape, lambda i, core: (0,) * len(a.shape))
    return pl.pallas_call(
        inner_kernel,
        grid_spec=pltpu.PrefetchScalarGridSpec(
            num_scalar_prefetch=1,
            grid=(1,),
            in_specs=[whole(acts), whole(mine), whole(other)],
            out_specs=pl.BlockSpec((acts.shape[0], rank), lambda i, core: (0, 0)),
            scratch_shapes=[pltpu.VMEM((acts.shape[1], rank), BF16)],
        ),
        out_shape=jax.ShapeDtypeStruct((acts.shape[0], rank), F32),
        compiler_params=pltpu.CompilerParams(vmem_limit_bytes=40 * MIB),
        name="inner",
    )(core, acts, mine, other)


def change_kernel(*refs):
    shares, basis_ref, out_ref = refs[:4], refs[4], refs[5]
    total = shares[0][...].astype(F32)
    for ref in shares[1:]:
        total += ref[...].astype(F32)
    zh, zl = two_terms(total)
    both = dot_t(jnp.concatenate([zh, zl], axis=0), basis_ref[...], ((1,), (1,)))
    out_ref[...] = (learning_rate * (both[: zh.shape[0]] + both[zh.shape[0] :])).astype(BF16)


def change_of(shares, basis):
    columns = 1024
    tokens, rank = shares[0].shape
    return pl.pallas_call(
        change_kernel,
        grid=(2,),
        in_specs=[pl.BlockSpec((tokens, rank), lambda i: (0, 0))] * 4
        + [pl.BlockSpec((columns, rank), lambda i: (i, 0))],
        out_specs=pl.BlockSpec((tokens, columns), lambda i: (0, i)),
        out_shape=jax.ShapeDtypeStruct((tokens, 2 * columns), BF16),
        compiler_params=pltpu.CompilerParams(vmem_limit_bytes=24 * MIB),
        name="change",
    )(*shares, basis)


def halves_kernel(first_ref, last_ref, *out_refs):
    out_refs[0][...] = first_ref[...]
    out_refs[1][...] = last_ref[...]


def halves(first, last):
    rows, width = first.shape
    shape = (rows // 2, width)
    return pl.pallas_call(
        halves_kernel,
        grid=(1,),
        in_specs=[pl.BlockSpec(shape, lambda i: (0, 0)), pl.BlockSpec(shape, lambda i: (1, 0))],
        out_specs=[pl.BlockSpec(shape, lambda i: (0, 0))] * 2,
        out_shape=[jax.ShapeDtypeStruct(shape, BF16)] * 2,
        compiler_params=pltpu.CompilerParams(vmem_limit_bytes=16 * MIB),
        name="halves",
    )(first, last)


def output_kernel(part_ref, change_ref, out_ref):
    for n in range(part_ref.shape[0]):
        columns = slice(n * 256, (n + 1) * 256)
        total = part_ref[n].astype(F32) - change_ref[:, columns].astype(F32)
        out_ref[:, columns] = total.astype(BF16)


def output_rows(part, change):
    blocks, tokens, columns = part.shape
    return pl.pallas_call(
        output_kernel,
        grid=(2,),
        in_specs=[
            pl.BlockSpec((blocks // 2, tokens, columns), lambda i: (i, 0, 0)),
            pl.BlockSpec((tokens, blocks // 2 * columns), lambda i: (0, i)),
        ],
        out_specs=pl.BlockSpec((tokens, blocks // 2 * columns), lambda i: (0, i)),
        out_shape=jax.ShapeDtypeStruct((tokens, blocks * columns), BF16),
        compiler_params=pltpu.CompilerParams(vmem_limit_bytes=24 * MIB),
        name="output_rows",
    )(part, change)


def swap(value):
    return lax.ppermute(value, "c", [(0, 1), (1, 0)])


def shift(value, axis, by):
    return lax.ppermute(value, axis, [(i, (i + by) % 4) for i in range(4)])


def on_device(acts, out_grad, basis, moment1, moment2, weight, next_acts):
    z, x, c, y = (lax.axis_index(a).astype(jnp.int32) for a in ("z", "x", "c", "y"))
    core, tensor = c[None], y[None]
    old = weight[0]
    keep, give = project(core, acts, out_grad, basis)
    own = lax.all_to_all(exchange_order(ORDER, tensor, old), ("x", "c"), 0, 0)
    got, beside = swap(give), swap(next_acts)
    rows = lax.dynamic_slice_in_dim(basis, y * 2048, 2048, axis=0).astype(BF16)
    place = [(v + d) % 4 for v in (z, x) for d in (0, 3, 1, 2)]
    place = jnp.stack(place[:4] + [2 * v + c for v in place[4:]] + [2 * v + 1 - c for v in place[4:]])
    own, keep, got, tokens, beside, rows, place = lax.optimization_barrier(
        (own, keep, got, next_acts, beside, rows, place)
    )
    own = own.reshape(512, 1024)
    near = (shift(own, "z", 1), shift(own, "z", -1), shift(tokens, "x", 1), shift(tokens, "x", -1))
    right, left, tr, tl = lax.optimization_barrier(near)
    ta, tb = halves(tr, tl)
    ta, tb, right, left = lax.optimization_barrier((ta, tb, right, left))
    near_a, near_b = halves(right, left)
    ta, tb = shift(ta, "x", 1), shift(tb, "x", -1)
    far_a, far_b = shift(near_a, "z", 1), shift(near_b, "z", -1)
    ta, tb, tr, tl, far_a, far_b = lax.optimization_barrier((ta, tb, tr, tl, far_a, far_b))
    pieces = (own, right, left, far_a, far_b)
    blocks = (tokens, tr, tl, ta, tb)
    others = (beside, *(swap(v) for v in blocks[1:]))
    up2, up1, up3, up0 = parts(place, pieces, blocks)
    got_up2, got_up3 = shift(up2, "y", 1), shift(up3, "y", -1)
    down2, down1, down3, down0 = parts(place, pieces, others)
    got_down1, got_down2 = shift(down1, "y", 1), shift(down2, "y", -1)
    keep, got, down2 = lax.optimization_barrier((keep, got, down2))
    projected = (keep + got.astype(F32)).astype(BF16)
    projected = lax.all_to_all(projected, ("z", "x"), 0, 0)
    up1, got_up3 = lax.optimization_barrier((up1, got_up3))
    up1, down3 = sums(((up1, got_up2), (down3, got_down2)))
    got_up1, got_down3 = shift(up1, "y", 1), shift(down3, "y", -1)
    projected, up1 = lax.optimization_barrier((projected, up1))
    first, second, direction, sent = optimizer_step(projected, moment1[0], moment2[0])
    mine = lax.all_to_all(sent, ("z", "x"), 0, 0)
    fresh = fresh_rows(direction, basis, old)
    up0, down0, fresh = lax.optimization_barrier((up0, down0, fresh))
    part = sums(((up0, got_up1, got_up3), (down0, got_down1, got_down3)), place)
    part, mine = lax.optimization_barrier((part, mine))
    share = inner(core, next_acts, mine, swap(mine)).astype(BF16)
    shares = [share] + [shift(share, "y", d) for d in (1, -1, 2)]
    change = change_of(shares, rows)
    part = lax.all_to_all(part, ("x", "c"), 0, 0)
    output = output_rows(part, change)
    return (output, fresh[None], first[None], second[None])


def solution(mesh):
    cube = Mesh(mesh.devices.reshape(4, 4, 2, 4), ("z", "x", "c", "y"))
    placed = (
        P(DP, "y"),
        P(DP, None),
        P(),
        P("y", DP, None),
        P("y", DP, None),
        P("y", DP, None),
        P(DP, "y"),
    )
    return jax.shard_map(
        on_device,
        mesh=cube,
        in_specs=placed,
        out_specs=(
            P(DP, "y"),
            P("y", DP, None),
            P("y", DP, None),
            P("y", DP, None),
        ),
        check_vma=False,
    )
```

```python
import functools

import jax
import jax.numpy as jnp
from jax import lax
from jax.experimental import pallas as pl
from jax.experimental.pallas import tpu as pltpu
from jax.sharding import Mesh
from jax.sharding import PartitionSpec as P

beta_one = 0.9
beta_two = 0.999
adam_step = 10.0
learning_rate = 0.02
epsilon = 1e-08

F32 = jnp.float32
BF16 = jnp.bfloat16
DP = ("z", "x", "c")
MIB = 1 << 20


def two_terms(value):
    high = value.astype(BF16)
    low = (value - high.astype(F32)).astype(BF16)
    return high, low


def dot(a, b):
    return jnp.dot(a, b, preferred_element_type=F32)


def dot_t(a, b, dims):
    return lax.dot_general(a, b, (dims, ((), ())), preferred_element_type=F32)


def project_kernel(core_ref, grad_ref, basis_ref, acts_ref, keep_ref, give_ref, total):
    step = pl.program_id(0)
    high, low = two_terms(basis_ref[...])
    grad = grad_ref[...]
    term = dot(grad, high) + dot(grad, low)

    @pl.when(step == 0)
    def _():
        total[...] = term

    @pl.when(step > 0)
    def _():
        total[...] += term

    @pl.when(step == pl.num_programs(0) - 1)
    def _():
        high, low = two_terms(total[...])
        acts = acts_ref[...]
        term = dot_t(acts, high, ((0,), (0,))) + dot_t(acts, low, ((0,), (0,)))
        term = term.reshape(16, 2, 64, term.shape[-1])
        mine = core_ref[0] == 0
        keep_ref[...] = jnp.where(mine, term[:, 0], term[:, 1])
        give_ref[...] = jnp.where(mine, term[:, 1], term[:, 0]).astype(BF16)


def project(core, acts, out_grad, basis):
    steps = 8
    tokens, width = out_grad.shape
    rank = basis.shape[1]
    depth = width // steps
    return pl.pallas_call(
        project_kernel,
        grid_spec=pltpu.PrefetchScalarGridSpec(
            num_scalar_prefetch=1,
            grid=(steps,),
            in_specs=[
                pl.BlockSpec((tokens, depth), lambda i, core: (0, i)),
                pl.BlockSpec((depth, rank), lambda i, core: (i, 0)),
                pl.BlockSpec(acts.shape, lambda i, core: (0, 0)),
            ],
            out_specs=[pl.BlockSpec((16, 64, rank), lambda i, core: (0, 0, 0))] * 2,
            scratch_shapes=[pltpu.VMEM((tokens, rank), F32)],
        ),
        out_shape=[
            jax.ShapeDtypeStruct((16, 64, rank), F32),
            jax.ShapeDtypeStruct((16, 64, rank), BF16),
        ],
        compiler_params=pltpu.CompilerParams(vmem_limit_bytes=48 * MIB),
        name="project",
    )(core, out_grad, basis, acts)


ORDER = (2, 1, 3, 0)


def exchange_order_kernel(order, y_ref, weight_ref, out_ref, held, sems):
    loads = []
    for i, d in enumerate(order):
        column = pl.multiple_of(lax.rem(y_ref[0] + d, 4) * 2048, 2048)
        loads.append(pltpu.make_async_copy(weight_ref.at[:, pl.ds(column, 2048)], held.at[i], sems.at[i]))
    for copy in loads:
        copy.start()
    for i, copy in enumerate(loads):
        copy.wait()
        for k in range(8):
            out_ref[k, :, i * 256 : (i + 1) * 256] = held[i, :, k * 256 : (k + 1) * 256]


def exchange_order(order, y, weight):
    rows = weight.shape[0]
    count = len(order)
    return pl.pallas_call(
        functools.partial(exchange_order_kernel, order),
        in_specs=[pl.BlockSpec(memory_space=pltpu.SMEM), pl.BlockSpec(memory_space=pl.ANY)],
        out_shape=jax.ShapeDtypeStruct((8, rows, 256 * count), BF16),
        scratch_shapes=[pltpu.VMEM((count, rows, 2048), BF16), pltpu.SemaphoreType.DMA((count,))],
        compiler_params=pltpu.CompilerParams(vmem_limit_bytes=58 * MIB),
        name="exchange_order",
    )(y, weight)


def fresh_kernel(direction_ref, basis_ref, weight_ref, out_ref):
    dh, dl = two_terms(direction_ref[...])
    both = dot_t(jnp.concatenate([dh, dl], axis=0), basis_ref[...].astype(BF16), ((1,), (1,)))
    change = both[: dh.shape[0]] + both[dh.shape[0] :]
    out_ref[...] = (weight_ref[...].astype(F32) - learning_rate * change).astype(BF16)


def fresh_rows(direction, basis, weight):
    rows, width = weight.shape
    block = 2048
    return pl.pallas_call(
        fresh_kernel,
        grid=(width // block,),
        in_specs=[
            pl.BlockSpec(direction.shape, lambda i: (0, 0)),
            pl.BlockSpec((block, basis.shape[1]), lambda i: (i, 0)),
            pl.BlockSpec((rows, block), lambda i: (0, i)),
        ],
        out_specs=pl.BlockSpec((rows, block), lambda i: (0, i)),
        out_shape=jax.ShapeDtypeStruct((rows, width), BF16),
        compiler_params=pltpu.CompilerParams(vmem_limit_bytes=48 * MIB),
        name="fresh_rows",
    )(direction, basis, weight)


def parts_kernel(place_ref, *refs):
    pieces, acts, outs = refs[:5], refs[5:10], refs[10:14]
    rows, tokens, made, row_sems, token_sems, made_sems = refs[14:]
    depth, size = pieces[0].shape[0], tokens.shape[1]
    half = size // 2

    loads = []
    for n, (index, shift) in enumerate(((0, 0), (1, 0), (2, 0), (3, 0), (3, depth // 2))):
        count = pieces[n].shape[0]
        at = pl.ds(pl.multiple_of(place_ref[index] * depth + shift, count), count)
        loads.append(pltpu.make_async_copy(pieces[n], rows.at[at, :], row_sems.at[n]))
    token_loads = [[pltpu.make_async_copy(acts[n], tokens.at[n], token_sems.at[n])] for n in range(3)]
    token_loads.append(
        [
            pltpu.make_async_copy(acts[3 + m], tokens.at[3, m * half : (m + 1) * half, :], token_sems.at[3 + m])
            for m in range(2)
        ]
    )
    for copy in loads + token_loads[0]:
        copy.start()
    for copy in loads:
        copy.wait()
    stores = []
    for n in range(4):
        if n < 3:
            for copy in token_loads[n + 1]:
                copy.start()
        for copy in token_loads[n]:
            copy.wait()
        part = dot(tokens[n], rows[...]).astype(BF16)
        for i in range(4):
            made[n, i] = part[:, i * 256 : (i + 1) * 256]
            stores.append(pltpu.make_async_copy(made.at[n, i], outs[i].at[n], made_sems.at[n, i]))
            stores[-1].start()
    for copy in stores:
        copy.wait()


def parts(place, pieces, acts):
    tokens, depth = acts[0].shape
    whole = pl.BlockSpec(memory_space=pl.ANY)
    return pl.pallas_call(
        parts_kernel,
        in_specs=[pl.BlockSpec(memory_space=pltpu.SMEM)] + [whole] * 10,
        out_specs=[whole] * 4,
        scratch_shapes=[
            pltpu.VMEM((depth, pieces[0].shape[1]), BF16),
            pltpu.VMEM((4, tokens, depth), BF16),
            pltpu.VMEM((4, 4, tokens, 256), BF16),
            pltpu.SemaphoreType.DMA((5,)),
            pltpu.SemaphoreType.DMA((5,)),
            pltpu.SemaphoreType.DMA((4, 4)),
        ],
        out_shape=[jax.ShapeDtypeStruct((4, tokens, 256), BF16)] * 4,
        compiler_params=pltpu.CompilerParams(vmem_limit_bytes=58 * MIB),
        name="parts",
    )(place, *pieces, *acts)


def sums_kernel(groups, terms, placed, *refs):
    place_ref, refs = (refs[0], refs[1:]) if placed else (None, refs)
    ins, outs = refs[: groups * terms], refs[groups * terms : -4]
    held, made, in_sems, out_sems = refs[-4:]
    loads = [pltpu.make_async_copy(ins[k], held.at[k], in_sems.at[k]) for k in range(groups * terms)]
    for copy in loads:
        copy.start()
    stores = []
    for g in range(groups):
        for k in range(terms):
            loads[g * terms + k].wait()
        for n in range(4):
            total = held[g * terms, n].astype(F32)
            for k in range(1, terms):
                total += held[g * terms + k, n].astype(F32)
            made[g, n] = total.astype(BF16)
            target = outs[0].at[place_ref[4 + 4 * g + n]] if placed else outs[g].at[n]
            stores.append(pltpu.make_async_copy(made.at[g, n], target, out_sems.at[g, n]))
            stores[-1].start()
    for copy in stores:
        copy.wait()


def sums(groups, place=None):
    count, terms, block = len(groups), len(groups[0]), groups[0][0].shape
    whole = pl.BlockSpec(memory_space=pl.ANY)
    placed = place is not None
    shape = jax.ShapeDtypeStruct((4 * count, *block[1:]) if placed else block, BF16)
    return pl.pallas_call(
        functools.partial(sums_kernel, count, terms, placed),
        in_specs=[pl.BlockSpec(memory_space=pltpu.SMEM)] * placed + [whole] * (count * terms),
        out_specs=whole if placed else [whole] * count,
        out_shape=shape if placed else [shape] * count,
        scratch_shapes=[
            pltpu.VMEM((count * terms, *block), BF16),
            pltpu.VMEM((count, *block), BF16),
            pltpu.SemaphoreType.DMA((count * terms,)),
            pltpu.SemaphoreType.DMA((count, 4)),
        ],
        compiler_params=pltpu.CompilerParams(vmem_limit_bytes=58 * MIB),
        name="sums",
    )(*[place] * placed, *[v for g in groups for v in g])


def step_kernel(terms_ref, one_ref, two_ref, first_ref, second_ref, direction_ref, sent_ref):
    projected = jnp.sum(terms_ref[...].astype(F32), axis=0)
    first = beta_one * one_ref[...] + (1.0 - beta_one) * projected
    second = beta_two * two_ref[...] + (1.0 - beta_two) * projected * projected
    direction = (
        first
        / (1.0 - beta_one**adam_step)
        / (jnp.sqrt(second / (1.0 - beta_two**adam_step)) + epsilon)
    )
    first_ref[...] = first
    second_ref[...] = second
    direction_ref[...] = direction
    sent_ref[...] = jnp.broadcast_to(direction.astype(BF16)[None], sent_ref.shape)


def optimizer_step(terms, one, two):
    shape = jax.ShapeDtypeStruct(one.shape, F32)
    return pl.pallas_call(
        step_kernel,
        out_shape=[shape] * 3 + [jax.ShapeDtypeStruct(terms.shape, BF16)],
        compiler_params=pltpu.CompilerParams(vmem_limit_bytes=16 * MIB),
        name="optimizer_step",
    )(terms, one, two)


def inner_kernel(core_ref, acts_ref, mine_ref, other_ref, out_ref, rows):
    for k in range(16):
        for ref, core in ((mine_ref, core_ref[0]), (other_ref, 1 - core_ref[0])):
            at = pl.ds(pl.multiple_of(k * 128 + core * 64, 64), 64)
            rows[at, :] = ref[k]
    out_ref[...] = dot(acts_ref[...], rows[...])


def inner(core, acts, mine, other):
    rank = mine.shape[-1]
    whole = lambda a: pl.BlockSpec(a.shape, lambda i, core: (0,) * len(a.shape))
    return pl.pallas_call(
        inner_kernel,
        grid_spec=pltpu.PrefetchScalarGridSpec(
            num_scalar_prefetch=1,
            grid=(1,),
            in_specs=[whole(acts), whole(mine), whole(other)],
            out_specs=pl.BlockSpec((acts.shape[0], rank), lambda i, core: (0, 0)),
            scratch_shapes=[pltpu.VMEM((acts.shape[1], rank), BF16)],
        ),
        out_shape=jax.ShapeDtypeStruct((acts.shape[0], rank), F32),
        compiler_params=pltpu.CompilerParams(vmem_limit_bytes=40 * MIB),
        name="inner",
    )(core, acts, mine, other)


def change_kernel(*refs):
    shares, basis_ref, out_ref = refs[:4], refs[4], refs[5]
    total = shares[0][...].astype(F32)
    for ref in shares[1:]:
        total += ref[...].astype(F32)
    zh, zl = two_terms(total)
    both = dot_t(jnp.concatenate([zh, zl], axis=0), basis_ref[...], ((1,), (1,)))
    out_ref[...] = (learning_rate * (both[: zh.shape[0]] + both[zh.shape[0] :])).astype(BF16)


def change_of(shares, basis):
    columns = 1024
    tokens, rank = shares[0].shape
    return pl.pallas_call(
        change_kernel,
        grid=(2,),
        in_specs=[pl.BlockSpec((tokens, rank), lambda i: (0, 0))] * 4
        + [pl.BlockSpec((columns, rank), lambda i: (i, 0))],
        out_specs=pl.BlockSpec((tokens, columns), lambda i: (0, i)),
        out_shape=jax.ShapeDtypeStruct((tokens, 2 * columns), BF16),
        compiler_params=pltpu.CompilerParams(vmem_limit_bytes=24 * MIB),
        name="change",
    )(*shares, basis)


def halves_kernel(first_ref, last_ref, *out_refs):
    out_refs[0][...] = first_ref[...]
    out_refs[1][...] = last_ref[...]


def halves(first, last):
    rows, width = first.shape
    shape = (rows // 2, width)
    return pl.pallas_call(
        halves_kernel,
        grid=(1,),
        in_specs=[pl.BlockSpec(shape, lambda i: (0, 0)), pl.BlockSpec(shape, lambda i: (1, 0))],
        out_specs=[pl.BlockSpec(shape, lambda i: (0, 0))] * 2,
        out_shape=[jax.ShapeDtypeStruct(shape, BF16)] * 2,
        compiler_params=pltpu.CompilerParams(vmem_limit_bytes=16 * MIB),
        name="halves",
    )(first, last)


def output_kernel(part_ref, change_ref, out_ref):
    for n in range(part_ref.shape[0]):
        columns = slice(n * 256, (n + 1) * 256)
        total = part_ref[n].astype(F32) - change_ref[:, columns].astype(F32)
        out_ref[:, columns] = total.astype(BF16)


def output_rows(part, change):
    blocks, tokens, columns = part.shape
    return pl.pallas_call(
        output_kernel,
        grid=(2,),
        in_specs=[
            pl.BlockSpec((blocks // 2, tokens, columns), lambda i: (i, 0, 0)),
            pl.BlockSpec((tokens, blocks // 2 * columns), lambda i: (0, i)),
        ],
        out_specs=pl.BlockSpec((tokens, blocks // 2 * columns), lambda i: (0, i)),
        out_shape=jax.ShapeDtypeStruct((tokens, blocks * columns), BF16),
        compiler_params=pltpu.CompilerParams(vmem_limit_bytes=24 * MIB),
        name="output_rows",
    )(part, change)


def swap(value):
    return lax.ppermute(value, "c", [(0, 1), (1, 0)])


def shift(value, axis, by):
    return lax.ppermute(value, axis, [(i, (i + by) % 4) for i in range(4)])


def on_device(acts, out_grad, basis, moment1, moment2, weight, next_acts):
    z, x, c, y = (lax.axis_index(a).astype(jnp.int32) for a in ("z", "x", "c", "y"))
    core, tensor = c[None], y[None]
    old = weight[0]
    keep, give = project(core, acts, out_grad, basis)
    own = lax.all_to_all(exchange_order(ORDER, tensor, old), ("x", "c"), 0, 0)
    got, beside = swap(give), swap(next_acts)
    place = [(v + d) % 4 for v in (z, x) for d in (0, 3, 1, 2)]
    place = jnp.stack(place[:4] + [2 * v + c for v in place[4:]] + [2 * v + 1 - c for v in place[4:]])
    keep, got, tokens, beside, place, rows = lax.optimization_barrier(
        (keep, got, next_acts, beside, place, basis)
    )
    own = own.reshape(512, 1024)
    near = (shift(own, "z", 1), shift(own, "z", -1), shift(tokens, "x", 1), shift(tokens, "x", -1))
    rows = lax.dynamic_slice_in_dim(rows, y * 2048, 2048, axis=0).astype(BF16)
    projected = (keep + got.astype(F32)).astype(BF16)
    right, left, tr, tl, rows, projected = lax.optimization_barrier((*near, rows, projected))
    ta, tb = halves(tr, tl)
    ta, tb, right, left = lax.optimization_barrier((ta, tb, right, left))
    near_a, near_b = halves(right, left)
    ta, tb = shift(ta, "x", 1), shift(tb, "x", -1)
    far_a, far_b = shift(near_a, "z", 1), shift(near_b, "z", -1)
    ta, tb, tr, tl, far_a, far_b = lax.optimization_barrier((ta, tb, tr, tl, far_a, far_b))
    pieces = (own, right, left, far_a, far_b)
    blocks = (tokens, tr, tl, ta, tb)
    others = (beside, *(swap(v) for v in blocks[1:]))
    up2, up1, up3, up0 = parts(place, pieces, blocks)
    got_up2, got_up3 = shift(up2, "y", 1), shift(up3, "y", -1)
    down2, down1, down3, down0 = parts(place, pieces, others)
    got_down1, got_down2 = shift(down1, "y", 1), shift(down2, "y", -1)
    projected, down2 = lax.optimization_barrier((projected, down2))
    projected = lax.all_to_all(projected, ("z", "x"), 0, 0)
    up1, got_up3 = lax.optimization_barrier((up1, got_up3))
    up1, down3 = sums(((up1, got_up2), (down3, got_down2)))
    got_up1, got_down3 = shift(up1, "y", 1), shift(down3, "y", -1)
    projected, up1 = lax.optimization_barrier((projected, up1))
    first, second, direction, sent = optimizer_step(projected, moment1[0], moment2[0])
    mine = lax.all_to_all(sent, ("z", "x"), 0, 0)
    fresh = fresh_rows(direction, basis, old)
    up0, down0, fresh = lax.optimization_barrier((up0, down0, fresh))
    part = sums(((up0, got_up1, got_up3), (down0, got_down1, got_down3)), place)
    part, mine = lax.optimization_barrier((part, mine))
    share = inner(core, next_acts, mine, swap(mine)).astype(BF16)
    shares = [share] + [shift(share, "y", d) for d in (1, -1, 2)]
    change = change_of(shares, rows)
    part = lax.all_to_all(part, ("x", "c"), 0, 0)
    output = output_rows(part, change)
    return (output, fresh[None], first[None], second[None])


def solution(mesh):
    cube = Mesh(mesh.devices.reshape(4, 4, 2, 4), ("z", "x", "c", "y"))
    placed = (
        P(DP, "y"),
        P(DP, None),
        P(),
        P("y", DP, None),
        P("y", DP, None),
        P("y", DP, None),
        P(DP, "y"),
    )
    return jax.shard_map(
        on_device,
        mesh=cube,
        in_specs=placed,
        out_specs=(
            P(DP, "y"),
            P("y", DP, None),
            P("y", DP, None),
            P("y", DP, None),
        ),
        check_vma=False,
    )
```

```python
import functools

import jax
import jax.numpy as jnp
from jax import lax
from jax.experimental import pallas as pl
from jax.experimental.pallas import tpu as pltpu
from jax.sharding import Mesh
from jax.sharding import PartitionSpec as P

beta_one = 0.9
beta_two = 0.999
adam_step = 10.0
learning_rate = 0.02
epsilon = 1e-08

F32 = jnp.float32
BF16 = jnp.bfloat16
DP = ("z", "x", "c")
MIB = 1 << 20


def two_terms(value):
    high = value.astype(BF16)
    low = (value - high.astype(F32)).astype(BF16)
    return high, low


def dot(a, b):
    return jnp.dot(a, b, preferred_element_type=F32)


def dot_t(a, b, dims):
    return lax.dot_general(a, b, (dims, ((), ())), preferred_element_type=F32)


def project_kernel(core_ref, grad_ref, basis_ref, acts_ref, keep_ref, give_ref, total):
    step = pl.program_id(0)
    high, low = two_terms(basis_ref[...])
    grad = grad_ref[...]
    term = dot(grad, high) + dot(grad, low)

    @pl.when(step == 0)
    def _():
        total[...] = term

    @pl.when(step > 0)
    def _():
        total[...] += term

    @pl.when(step == pl.num_programs(0) - 1)
    def _():
        high, low = two_terms(total[...])
        acts = acts_ref[...]
        term = dot_t(acts, high, ((0,), (0,))) + dot_t(acts, low, ((0,), (0,)))
        term = term.reshape(16, 2, 64, term.shape[-1])
        mine = core_ref[0] == 0
        keep_ref[...] = jnp.where(mine, term[:, 0], term[:, 1])
        give_ref[...] = jnp.where(mine, term[:, 1], term[:, 0]).astype(BF16)


def project(core, acts, out_grad, basis):
    steps = 8
    tokens, width = out_grad.shape
    rank = basis.shape[1]
    depth = width // steps
    return pl.pallas_call(
        project_kernel,
        grid_spec=pltpu.PrefetchScalarGridSpec(
            num_scalar_prefetch=1,
            grid=(steps,),
            in_specs=[
                pl.BlockSpec((tokens, depth), lambda i, core: (0, i)),
                pl.BlockSpec((depth, rank), lambda i, core: (i, 0)),
                pl.BlockSpec(acts.shape, lambda i, core: (0, 0)),
            ],
            out_specs=[pl.BlockSpec((16, 64, rank), lambda i, core: (0, 0, 0))] * 2,
            scratch_shapes=[pltpu.VMEM((tokens, rank), F32)],
        ),
        out_shape=[
            jax.ShapeDtypeStruct((16, 64, rank), F32),
            jax.ShapeDtypeStruct((16, 64, rank), BF16),
        ],
        compiler_params=pltpu.CompilerParams(vmem_limit_bytes=48 * MIB),
        name="project",
    )(core, out_grad, basis, acts)


ORDER = (2, 1, 3, 0)


def exchange_order_kernel(order, y_ref, weight_ref, out_ref, held, sems):
    loads = []
    for i, d in enumerate(order):
        column = pl.multiple_of(lax.rem(y_ref[0] + d, 4) * 2048, 2048)
        loads.append(pltpu.make_async_copy(weight_ref.at[:, pl.ds(column, 2048)], held.at[i], sems.at[i]))
    for copy in loads:
        copy.start()
    for i, copy in enumerate(loads):
        copy.wait()
        for k in range(8):
            out_ref[k, :, i * 256 : (i + 1) * 256] = held[i, :, k * 256 : (k + 1) * 256]


def exchange_order(order, y, weight):
    rows = weight.shape[0]
    count = len(order)
    return pl.pallas_call(
        functools.partial(exchange_order_kernel, order),
        in_specs=[pl.BlockSpec(memory_space=pltpu.SMEM), pl.BlockSpec(memory_space=pl.ANY)],
        out_shape=jax.ShapeDtypeStruct((8, rows, 256 * count), BF16),
        scratch_shapes=[pltpu.VMEM((count, rows, 2048), BF16), pltpu.SemaphoreType.DMA((count,))],
        compiler_params=pltpu.CompilerParams(vmem_limit_bytes=58 * MIB),
        name="exchange_order",
    )(y, weight)


def fresh_kernel(direction_ref, basis_ref, weight_ref, out_ref):
    dh, dl = two_terms(direction_ref[...])
    both = dot_t(jnp.concatenate([dh, dl], axis=0), basis_ref[...].astype(BF16), ((1,), (1,)))
    change = both[: dh.shape[0]] + both[dh.shape[0] :]
    out_ref[...] = (weight_ref[...].astype(F32) - learning_rate * change).astype(BF16)


def fresh_rows(direction, basis, weight):
    rows, width = weight.shape
    block = 2048
    return pl.pallas_call(
        fresh_kernel,
        grid=(width // block,),
        in_specs=[
            pl.BlockSpec(direction.shape, lambda i: (0, 0)),
            pl.BlockSpec((block, basis.shape[1]), lambda i: (i, 0)),
            pl.BlockSpec((rows, block), lambda i: (0, i)),
        ],
        out_specs=pl.BlockSpec((rows, block), lambda i: (0, i)),
        out_shape=jax.ShapeDtypeStruct((rows, width), BF16),
        compiler_params=pltpu.CompilerParams(vmem_limit_bytes=48 * MIB),
        name="fresh_rows",
    )(direction, basis, weight)


def parts_kernel(place_ref, *refs):
    pieces, acts, outs = refs[:5], refs[5:10], refs[10:14]
    rows, tokens, made, row_sems, token_sems, made_sems = refs[14:]
    depth, size = pieces[0].shape[0], tokens.shape[1]
    half = size // 2

    loads = []
    for n, (index, shift) in enumerate(((0, 0), (1, 0), (2, 0), (3, 0), (3, depth // 2))):
        count = pieces[n].shape[0]
        at = pl.ds(pl.multiple_of(place_ref[index] * depth + shift, count), count)
        loads.append(pltpu.make_async_copy(pieces[n], rows.at[at, :], row_sems.at[n]))
    token_loads = [[pltpu.make_async_copy(acts[n], tokens.at[n], token_sems.at[n])] for n in range(3)]
    token_loads.append(
        [
            pltpu.make_async_copy(acts[3 + m], tokens.at[3, m * half : (m + 1) * half, :], token_sems.at[3 + m])
            for m in range(2)
        ]
    )
    for copy in loads + token_loads[0]:
        copy.start()
    for copy in loads:
        copy.wait()
    stores = []
    for n in range(4):
        if n < 3:
            for copy in token_loads[n + 1]:
                copy.start()
        for copy in token_loads[n]:
            copy.wait()
        part = dot(tokens[n], rows[...]).astype(BF16)
        for i in range(4):
            made[n, i] = part[:, i * 256 : (i + 1) * 256]
            stores.append(pltpu.make_async_copy(made.at[n, i], outs[i].at[n], made_sems.at[n, i]))
            stores[-1].start()
    for copy in stores:
        copy.wait()


def parts(place, pieces, acts):
    tokens, depth = acts[0].shape
    whole = pl.BlockSpec(memory_space=pl.ANY)
    return pl.pallas_call(
        parts_kernel,
        in_specs=[pl.BlockSpec(memory_space=pltpu.SMEM)] + [whole] * 10,
        out_specs=[whole] * 4,
        scratch_shapes=[
            pltpu.VMEM((depth, pieces[0].shape[1]), BF16),
            pltpu.VMEM((4, tokens, depth), BF16),
            pltpu.VMEM((4, 4, tokens, 256), BF16),
            pltpu.SemaphoreType.DMA((5,)),
            pltpu.SemaphoreType.DMA((5,)),
            pltpu.SemaphoreType.DMA((4, 4)),
        ],
        out_shape=[jax.ShapeDtypeStruct((4, tokens, 256), BF16)] * 4,
        compiler_params=pltpu.CompilerParams(vmem_limit_bytes=58 * MIB),
        name="parts",
    )(place, *pieces, *acts)


def sums_kernel(groups, terms, placed, *refs):
    place_ref, refs = (refs[0], refs[1:]) if placed else (None, refs)
    ins, outs = refs[: groups * terms], refs[groups * terms : -4]
    held, made, in_sems, out_sems = refs[-4:]
    loads = [pltpu.make_async_copy(ins[k], held.at[k], in_sems.at[k]) for k in range(groups * terms)]
    for copy in loads:
        copy.start()
    stores = []
    for g in range(groups):
        for k in range(terms):
            loads[g * terms + k].wait()
        for n in range(4):
            total = held[g * terms, n].astype(F32)
            for k in range(1, terms):
                total += held[g * terms + k, n].astype(F32)
            made[g, n] = total.astype(BF16)
            target = outs[0].at[place_ref[4 + 4 * g + n]] if placed else outs[g].at[n]
            stores.append(pltpu.make_async_copy(made.at[g, n], target, out_sems.at[g, n]))
            stores[-1].start()
    for copy in stores:
        copy.wait()


def sums(groups, place=None):
    count, terms, block = len(groups), len(groups[0]), groups[0][0].shape
    whole = pl.BlockSpec(memory_space=pl.ANY)
    placed = place is not None
    shape = jax.ShapeDtypeStruct((4 * count, *block[1:]) if placed else block, BF16)
    return pl.pallas_call(
        functools.partial(sums_kernel, count, terms, placed),
        in_specs=[pl.BlockSpec(memory_space=pltpu.SMEM)] * placed + [whole] * (count * terms),
        out_specs=whole if placed else [whole] * count,
        out_shape=shape if placed else [shape] * count,
        scratch_shapes=[
            pltpu.VMEM((count * terms, *block), BF16),
            pltpu.VMEM((count, *block), BF16),
            pltpu.SemaphoreType.DMA((count * terms,)),
            pltpu.SemaphoreType.DMA((count, 4)),
        ],
        compiler_params=pltpu.CompilerParams(vmem_limit_bytes=58 * MIB),
        name="sums",
    )(*[place] * placed, *[v for g in groups for v in g])


def step_kernel(terms_ref, one_ref, two_ref, first_ref, second_ref, direction_ref, sent_ref):
    projected = jnp.sum(terms_ref[...].astype(F32), axis=0)
    first = beta_one * one_ref[...] + (1.0 - beta_one) * projected
    second = beta_two * two_ref[...] + (1.0 - beta_two) * projected * projected
    direction = (
        first
        / (1.0 - beta_one**adam_step)
        / (jnp.sqrt(second / (1.0 - beta_two**adam_step)) + epsilon)
    )
    first_ref[...] = first
    second_ref[...] = second
    direction_ref[...] = direction
    sent_ref[...] = jnp.broadcast_to(direction.astype(BF16)[None], sent_ref.shape)


def optimizer_step(terms, one, two):
    shape = jax.ShapeDtypeStruct(one.shape, F32)
    return pl.pallas_call(
        step_kernel,
        out_shape=[shape] * 3 + [jax.ShapeDtypeStruct(terms.shape, BF16)],
        compiler_params=pltpu.CompilerParams(vmem_limit_bytes=16 * MIB),
        name="optimizer_step",
    )(terms, one, two)


def inner_kernel(core_ref, acts_ref, mine_ref, other_ref, out_ref, rows):
    for k in range(16):
        for ref, core in ((mine_ref, core_ref[0]), (other_ref, 1 - core_ref[0])):
            at = pl.ds(pl.multiple_of(k * 128 + core * 64, 64), 64)
            rows[at, :] = ref[k]
    out_ref[...] = dot(acts_ref[...], rows[...])


def inner(core, acts, mine, other):
    rank = mine.shape[-1]
    whole = lambda a: pl.BlockSpec(a.shape, lambda i, core: (0,) * len(a.shape))
    return pl.pallas_call(
        inner_kernel,
        grid_spec=pltpu.PrefetchScalarGridSpec(
            num_scalar_prefetch=1,
            grid=(1,),
            in_specs=[whole(acts), whole(mine), whole(other)],
            out_specs=pl.BlockSpec((acts.shape[0], rank), lambda i, core: (0, 0)),
            scratch_shapes=[pltpu.VMEM((acts.shape[1], rank), BF16)],
        ),
        out_shape=jax.ShapeDtypeStruct((acts.shape[0], rank), F32),
        compiler_params=pltpu.CompilerParams(vmem_limit_bytes=40 * MIB),
        name="inner",
    )(core, acts, mine, other)


def change_kernel(*refs):
    shares, basis_ref, out_ref = refs[:4], refs[4], refs[5]
    total = shares[0][...].astype(F32)
    for ref in shares[1:]:
        total += ref[...].astype(F32)
    zh, zl = two_terms(total)
    both = dot_t(jnp.concatenate([zh, zl], axis=0), basis_ref[...], ((1,), (1,)))
    out_ref[...] = (learning_rate * (both[: zh.shape[0]] + both[zh.shape[0] :])).astype(BF16)


def change_of(shares, basis):
    columns = 1024
    tokens, rank = shares[0].shape
    return pl.pallas_call(
        change_kernel,
        grid=(2,),
        in_specs=[pl.BlockSpec((tokens, rank), lambda i: (0, 0))] * 4
        + [pl.BlockSpec((columns, rank), lambda i: (i, 0))],
        out_specs=pl.BlockSpec((tokens, columns), lambda i: (0, i)),
        out_shape=jax.ShapeDtypeStruct((tokens, 2 * columns), BF16),
        compiler_params=pltpu.CompilerParams(vmem_limit_bytes=24 * MIB),
        name="change",
    )(*shares, basis)


def halves_kernel(first_ref, last_ref, *out_refs):
    out_refs[0][...] = first_ref[...]
    out_refs[1][...] = last_ref[...]


def halves(first, last):
    rows, width = first.shape
    shape = (rows // 2, width)
    return pl.pallas_call(
        halves_kernel,
        grid=(1,),
        in_specs=[pl.BlockSpec(shape, lambda i: (0, 0)), pl.BlockSpec(shape, lambda i: (1, 0))],
        out_specs=[pl.BlockSpec(shape, lambda i: (0, 0))] * 2,
        out_shape=[jax.ShapeDtypeStruct(shape, BF16)] * 2,
        compiler_params=pltpu.CompilerParams(vmem_limit_bytes=16 * MIB),
        name="halves",
    )(first, last)


def output_kernel(part_ref, change_ref, out_ref):
    for n in range(part_ref.shape[0]):
        columns = slice(n * 256, (n + 1) * 256)
        total = part_ref[n].astype(F32) - change_ref[:, columns].astype(F32)
        out_ref[:, columns] = total.astype(BF16)


def output_rows(part, change):
    blocks, tokens, columns = part.shape
    return pl.pallas_call(
        output_kernel,
        grid=(2,),
        in_specs=[
            pl.BlockSpec((blocks // 2, tokens, columns), lambda i: (i, 0, 0)),
            pl.BlockSpec((tokens, blocks // 2 * columns), lambda i: (0, i)),
        ],
        out_specs=pl.BlockSpec((tokens, blocks // 2 * columns), lambda i: (0, i)),
        out_shape=jax.ShapeDtypeStruct((tokens, blocks * columns), BF16),
        compiler_params=pltpu.CompilerParams(vmem_limit_bytes=24 * MIB),
        name="output_rows",
    )(part, change)


def swap(value):
    return lax.ppermute(value, "c", [(0, 1), (1, 0)])


def shift(value, axis, by):
    return lax.ppermute(value, axis, [(i, (i + by) % 4) for i in range(4)])


def on_device(acts, out_grad, basis, moment1, moment2, weight, next_acts):
    z, x, c, y = (lax.axis_index(a).astype(jnp.int32) for a in ("z", "x", "c", "y"))
    core, tensor = c[None], y[None]
    old = weight[0]
    keep, give = project(core, acts, out_grad, basis)
    own = lax.all_to_all(exchange_order(ORDER, tensor, old), ("x", "c"), 0, 0)
    got, beside = swap(give), swap(next_acts)
    place = [(v + d) % 4 for v in (z, x) for d in (0, 3, 1, 2)]
    place = jnp.stack(place[:4] + [2 * v + c for v in place[4:]] + [2 * v + 1 - c for v in place[4:]])
    keep, got, tokens, beside, place, rows = lax.optimization_barrier(
        (keep, got, next_acts, beside, place, basis)
    )
    own = own.reshape(512, 1024)
    near = (shift(own, "z", 1), shift(own, "z", -1), shift(tokens, "x", 1), shift(tokens, "x", -1))
    rows = lax.dynamic_slice_in_dim(rows, y * 2048, 2048, axis=0).astype(BF16)
    projected = (keep + got.astype(F32)).astype(BF16)
    right, left, tr, tl, rows, projected = lax.optimization_barrier((*near, rows, projected))
    ta, tb = halves(tr, tl)
    ta, tb, right, left = lax.optimization_barrier((ta, tb, right, left))
    near_a, near_b = halves(right, left)
    ta, tb = shift(ta, "x", 1), shift(tb, "x", -1)
    far_a, far_b = shift(near_a, "z", 1), shift(near_b, "z", -1)
    ta, tb, tr, tl, far_a, far_b = lax.optimization_barrier((ta, tb, tr, tl, far_a, far_b))
    pieces = (own, right, left, far_a, far_b)
    blocks = (tokens, tr, tl, ta, tb)
    others = (beside, *(swap(v) for v in blocks[1:]))
    up2, up1, up3, up0 = parts(place, pieces, blocks)
    got_up2, got_up3 = shift(up2, "y", 1), shift(up3, "y", -1)
    down2, down1, down3, down0 = parts(place, pieces, others)
    got_down1, got_down2 = shift(down1, "y", 1), shift(down2, "y", -1)
    projected, down2 = lax.optimization_barrier((projected, down2))
    projected = lax.all_to_all(projected, ("z", "x"), 0, 0)
    up1, got_up3 = lax.optimization_barrier((up1, got_up3))
    up1, down3 = sums(((up1, got_up2), (down3, got_down2)))
    got_up1, got_down3 = shift(up1, "y", 1), shift(down3, "y", -1)
    projected, up1 = lax.optimization_barrier((projected, up1))
    first, second, direction, sent = optimizer_step(projected, moment1[0], moment2[0])
    mine = lax.all_to_all(sent, ("z", "x"), 0, 0)
    up0, down0, direction = lax.optimization_barrier((up0, down0, direction))
    up0, down0 = sums(((up0, got_up3), (down0, got_down1)))
    part = sums(((up0, got_up1), (down0, got_down3)), place)
    part, mine = lax.optimization_barrier((part, mine))
    share = inner(core, next_acts, mine, swap(mine)).astype(BF16)
    shares = [share] + [shift(share, "y", d) for d in (1, -1, 2)]
    change = change_of(shares, rows)
    direction, mine = lax.optimization_barrier((direction, mine))
    fresh = fresh_rows(direction, basis, old)
    part = lax.all_to_all(part, ("x", "c"), 0, 0)
    output = output_rows(part, change)
    return (output, fresh[None], first[None], second[None])


def solution(mesh):
    cube = Mesh(mesh.devices.reshape(4, 4, 2, 4), ("z", "x", "c", "y"))
    placed = (
        P(DP, "y"),
        P(DP, None),
        P(),
        P("y", DP, None),
        P("y", DP, None),
        P("y", DP, None),
        P(DP, "y"),
    )
    return jax.shard_map(
        on_device,
        mesh=cube,
        in_specs=placed,
        out_specs=(
            P(DP, "y"),
            P("y", DP, None),
            P("y", DP, None),
            P("y", DP, None),
        ),
        check_vma=False,
    )
```
